32 devices in a mesh: dp: 16 (over z, y, core), mp: 2 (over x).
Axes of the slice: x: 2, y: 2, z: 4, core: 2. Of those that a mesh axis runs over, the one named last changes fastest.
Arguments:
- acts: bfloat16 [4096, 28672], P('dp', 'mp'), may hold values from -24 to 24
- grads: bfloat16 [4096, 8192], P('dp', 'mp'), may hold values from -6 to 6
- basis_in: bfloat16 [28672, 640], P('mp', 'dp'), may hold values from -0.03125 to 0.03125
- basis_out: bfloat16 [8192, 1024], P('dp', 'mp'), may hold values from -0.0625 to 0.0625
- damping: float32 [1], replicated, may hold values from 0.5 to 2
Outputs:
- update: bfloat16 [28672, 8192], P('mp', 'dp')
- diag: float32 [640, 1024], P('mp', 'dp')
The draws below stay inside these ranges and needn't reach their ends.
All inputs are finite; a program needn't handle non-finite values.
Results may differ from the reference program's by a relative error of at most 0.0085.
Values may be sent and summed in bfloat16 or wider, within the bound.
No kernel may reach another device: no remote copies, remote signals or barrier semaphores. Data moves between devices by JAX's collectives and lax.ppermute only.
A program may use at most 128 MiB of HBM per device.

```python
import math
import jax
import jax.numpy as jnp

DIN = 28672
DOUT = 8192
KA = 640
KG = 1024
TOKENS = 4096


def draw_acts(key, part):
    k_base, k_rows, k_cols = jax.random.split(key, 3)
    base = jax.random.normal(k_base, (TOKENS, DIN), jnp.float32)
    rows = jnp.exp(jax.random.uniform(k_rows, (TOKENS, 1), jnp.float32) * math.log(10.0)) / 4.6
    base = jnp.clip(base, -6.0, 6.0)
    cols = jnp.exp(jax.random.uniform(k_cols, (1, DIN), jnp.float32) * math.log(4.0)) / 2.3
    return (base * rows * cols).astype(jnp.bfloat16)


def levels(key, shape, cuts, least, top_value):
    loudness = 1.0
    for position, shards_of in cuts:
        steps = jax.random.uniform(jax.random.fold_in(jax.random.fold_in(key, 6), position), (shards_of,), jnp.float32, least / len(cuts), top_value / len(cuts))
        loudness = loudness * jnp.repeat(jnp.exp(steps), shape[position] // shards_of).reshape((-1,) + (1,) * (len(shape) - 1 - position))
    return loudness


def centred(key, dims, deviation, limit, cuts=(), dtype=jnp.bfloat16):
    loudness = levels(key, dims, cuts, -0.22, 0.18) if cuts else 1.0
    array = jax.random.normal(key, dims, jnp.float32) * deviation * loudness
    return jnp.minimum(jnp.maximum(array, -limit), limit).astype(dtype)


def setup_inputs(seed: int = 0) -> dict:
    arg_keys = jax.random.split(jax.random.key(seed), 6)
    return {
        "acts": draw_acts(jax.random.fold_in(arg_keys[5], 71), 0),
        "grads": centred(arg_keys[1], (TOKENS, DOUT), 1.0, 6.0, ((0, 16), (1, 2))),
        "basis_in": centred(arg_keys[2], (DIN, KA), DIN ** -0.5, 0.03125, ((0, 2), (1, 16))),
        "basis_out": centred(arg_keys[3], (DOUT, KG), DOUT ** -0.5, 0.0625, ((0, 16), (1, 2))),
        "damping": jnp.clip(jnp.exp(jax.random.uniform(arg_keys[4], (1,), jnp.float32, math.log(0.5), math.log(2.0))), 0.5, 2.0),
    }


def reference(acts, grads, basis_in, basis_out, damping):
    act_proj = jnp.dot(acts, basis_in, preferred_element_type=jnp.float32).astype(jnp.bfloat16)
    grad_proj = jnp.dot(grads, basis_out, preferred_element_type=jnp.float32).astype(jnp.bfloat16)
    act_sq = (act_proj.astype(jnp.float32) ** 2).astype(jnp.bfloat16)
    grad_sq = (grad_proj.astype(jnp.float32) ** 2).astype(jnp.bfloat16)
    grad_rot = jnp.dot(act_proj.T, grad_proj, preferred_element_type=jnp.float32)
    diag = jnp.dot(act_sq.T, grad_sq, preferred_element_type=jnp.float32) / TOKENS
    scaled = (grad_rot / (diag + damping[0])).astype(jnp.bfloat16)
    back = jnp.dot(scaled, basis_out.T, preferred_element_type=jnp.float32).astype(jnp.bfloat16)
    update = jnp.dot(basis_in, back, preferred_element_type=jnp.float32).astype(jnp.bfloat16)
    return update, diag
```

```python
import functools

import jax
import jax.numpy as jnp
from jax import lax
from jax.experimental import pallas as pl
from jax.experimental.pallas import tpu as pltpu
from jax.sharding import PartitionSpec as P

BF16, F32 = jnp.bfloat16, jnp.float32
VMEM_BYTES = 40 * 1024 * 1024


def flip(x, axis_name, bit):
    size = lax.axis_size(axis_name)
    return lax.ppermute(x, axis_name, [(i, i ^ bit) for i in range(size)])


def bits(axis_name):
    size = lax.axis_size(axis_name)
    assert size & (size - 1) == 0
    return [1 << k for k in range(size.bit_length() - 1)]


def reduce_halving(x, axis_name, axis):
    me = lax.axis_index(axis_name)
    for bit in bits(axis_name):
        shape = x.shape
        x = x.reshape(shape[:axis] + (shape[axis] // 2, 2) + shape[axis + 1 :])
        side = (me // bit) % 2
        sent = lax.dynamic_index_in_dim(x, 1 - side, axis + 1, False).astype(BF16)
        kept = lax.dynamic_index_in_dim(x, side, axis + 1, False)
        x = kept + flip(sent, axis_name, bit).astype(F32)
    return lax.squeeze(x, (axis,))


def gather_doubling(x, axis_name):
    me = lax.axis_index(axis_name)
    x = x[None]
    for bit in reversed(bits(axis_name)):
        other = flip(x, axis_name, bit)
        side = (me // bit) % 2
        low = jnp.where(side == 0, x, other)
        high = jnp.where(side == 0, other, x)
        x = jnp.stack([low, high], axis=1).reshape((2 * x.shape[0],) + x.shape[1:])
    return x


def gather_ring(block, axis_name):
    size = lax.axis_size(axis_name)
    half = size // 2
    order = list(range(0, half, 2)) + list(range(half - 1, 0, -2))
    hops = [(order[k], order[(k + 1) % half]) for k in range(half)]
    ahead = [[(2 * s + c, 2 * d + c) for s, d in hops] for c in (0, 1)]
    back = [[(d, s) for s, d in part] for part in ahead]
    me = lax.axis_index(axis_name)
    core, pair = me % 2, me // 2
    place = jnp.where(pair % 2 == 0, pair // 2, half - (pair + 1) // 2)

    def began(step):
        p = (place - step) % half
        return 2 * jnp.where(p < half // 2, 2 * p, 2 * (half - p) - 1) + core

    got = [(block, me)]
    one, two = block, block
    for step in range(1, half // 2):
        one = lax.ppermute(one, axis_name, ahead[0] + ahead[1])
        two = lax.ppermute(two, axis_name, back[0] + back[1])
        got += [(one, began(step)), (two, began(-step))]
    last = lax.ppermute(jnp.where(core == 0, one, two), axis_name, ahead[0] + back[1])
    got.append((last, began(half // 2)))
    return [p for b, j in got for p in ((b, j), (flip(b, axis_name, 1), j ^ 1))]


def tile_of(extent, most):
    return max(t for t in range(128, most + 1, 128) if extent % t == 0)


def project_kernel(basis_ref, acts_ref, out_ref, total):
    @pl.when(pl.program_id(0) == 0)
    def _():
        total[...] = jnp.zeros_like(total)

    total[...] += lax.dot_general(
        basis_ref[...], acts_ref[...], (((1,), (1,)), ((), ())), preferred_element_type=F32
    )

    @pl.when(pl.program_id(0) == pl.num_programs(0) - 1)
    def _():
        out_ref[...] = total[...]


def project(basis_t, acts):
    rows, units = basis_t.shape
    tokens = acts.shape[0]
    tile = tile_of(units, 2048)
    return pl.pallas_call(
        project_kernel,
        grid=(units // tile,),
        in_specs=[
            pl.BlockSpec((rows, tile), lambda i: (0, i)),
            pl.BlockSpec((tokens, tile), lambda i: (0, i)),
        ],
        out_specs=pl.BlockSpec((rows, tokens), lambda i: (0, 0)),
        out_shape=jax.ShapeDtypeStruct((rows, tokens), F32),
        scratch_shapes=[pltpu.VMEM((rows, tokens), F32)],
        compiler_params=pltpu.CompilerParams(vmem_limit_bytes=VMEM_BYTES),
        cost_estimate=pl.CostEstimate(
            flops=2 * rows * units * tokens, bytes_accessed=2 * units * (rows + tokens), transcendentals=0
        ),
        name="project_acts",
    )(basis_t, acts)


def update_kernel(basis_ref, back_ref, out_ref):
    out_ref[...] = lax.dot_general(
        basis_ref[...], back_ref[...], (((0,), (0,)), ((), ())), preferred_element_type=F32
    ).astype(out_ref.dtype)


def expand(basis_t, back):
    rows, units = basis_t.shape
    columns = back.shape[1]
    tile = tile_of(units, 1024)
    return pl.pallas_call(
        update_kernel,
        grid=(units // tile,),
        in_specs=[
            pl.BlockSpec((rows, tile), lambda i: (0, i)),
            pl.BlockSpec((rows, columns), lambda i: (0, 0)),
        ],
        out_specs=pl.BlockSpec((tile, columns), lambda i: (i, 0)),
        out_shape=jax.ShapeDtypeStruct((units, columns), BF16),
        compiler_params=pltpu.CompilerParams(vmem_limit_bytes=VMEM_BYTES),
        cost_estimate=pl.CostEstimate(
            flops=2 * rows * units * columns, bytes_accessed=2 * units * (rows + columns), transcendentals=0
        ),
        name="expand_update",
    )(basis_t, back)


def on_device(acts, grads, basis_in, basis_out, damping):
    tok_rows = acts.shape[0]
    n_dp, n_mp = lax.axis_size("dp"), lax.axis_size("mp")
    tokens_all = tok_rows * n_dp

    full_in_t = lax.all_gather(basis_in.T, "dp", axis=0, tiled=True)
    wide_grads = gather_doubling(grads, "mp")
    out_rows = gather_doubling(basis_out, "mp")
    out_units = basis_out.shape[0]
    grad_proj = jnp.zeros((tok_rows, basis_out.shape[1]), F32)
    for block, origin in gather_ring(basis_out, "dp"):
        part = origin * n_mp // n_dp
        first = (origin - part * (n_dp // n_mp)) * out_units
        columns = lax.dynamic_slice(wide_grads, (part, 0, first), (1, tok_rows, out_units))[0]
        grad_proj += jnp.dot(columns, block, preferred_element_type=F32)
    grad_proj = gather_doubling(grad_proj.astype(BF16), "mp")

    act_part = project(full_in_t, acts)
    act_part = act_part.reshape((n_mp, -1) + act_part.shape[1:])
    act_proj_t = reduce_halving(act_part, "mp", 0).astype(BF16)

    act_sq_t = (act_proj_t.astype(F32) ** 2).astype(BF16)
    grad_sq = (grad_proj.astype(F32) ** 2).astype(BF16)
    dims = (((1,), (1,)), ((), ()))

    def over_tokens(g, a):
        g = g.transpose(0, 2, 1)
        both = lax.dot_general(g.reshape((-1, tok_rows)), a, dims, preferred_element_type=F32)
        return both.reshape((n_dp, -1, a.shape[0]))

    partials = jnp.stack([over_tokens(grad_proj, act_proj_t), over_tokens(grad_sq, act_sq_t)])
    owned = reduce_halving(partials, "dp", 1)
    diag_t = owned[1] / tokens_all
    scaled_t = (owned[0] / (diag_t + damping[0])).astype(BF16)

    scaled_wide = gather_doubling(scaled_t, "dp").reshape((-1, scaled_t.shape[1]))
    rows_wide = out_rows.transpose(1, 0, 2).reshape((out_units, -1))
    back_part = lax.dot_general(
        scaled_wide, rows_wide, (((0,), (1,)), ((), ())), preferred_element_type=F32
    ).astype(BF16)
    back = gather_doubling(back_part, "mp").reshape((-1, out_units))
    return (expand(full_in_t, back), diag_t.T)


def solution(mesh):
    placed = (P("dp", "mp"), P("dp", "mp"), P("mp", "dp"), P("dp", "mp"), P())
    return jax.shard_map(
        on_device,
        mesh=mesh,
        in_specs=placed,
        out_specs=(P("mp", "dp"), P("mp", "dp")),
        check_vma=False,
    )
```

```python
import functools

import jax
import jax.numpy as jnp
from jax import lax
from jax.experimental import pallas as pl
from jax.experimental.pallas import tpu as pltpu
from jax.sharding import PartitionSpec as P

BF16, F32 = jnp.bfloat16, jnp.float32
VMEM_BYTES = 48 * 1024 * 1024
EXPAND_ROWS = 4096


def flip(x, axis_name, bit):
    size = lax.axis_size(axis_name)
    return lax.ppermute(x, axis_name, [(i, i ^ bit) for i in range(size)])


def bits(axis_name):
    size = lax.axis_size(axis_name)
    assert size & (size - 1) == 0
    return [1 << k for k in range(size.bit_length() - 1)]


def gather_doubling(x, axis_name):
    me = lax.axis_index(axis_name)
    x = x[None]
    for bit in reversed(bits(axis_name)):
        other = flip(x, axis_name, bit)
        side = (me // bit) % 2
        low = jnp.where(side == 0, x, other)
        high = jnp.where(side == 0, other, x)
        x = jnp.stack([low, high], axis=1).reshape((2 * x.shape[0],) + x.shape[1:])
    return x


def ring_hops(size):
    half = size // 2
    order = list(range(0, half, 2)) + list(range(half - 1, 0, -2))
    hops = [(order[k], order[(k + 1) % half]) for k in range(half)]
    ahead = [[(2 * s + c, 2 * d + c) for s, d in hops] for c in (0, 1)]
    return ahead, [[(d, s) for s, d in part] for part in ahead]


def ring_place(axis_name):
    half = lax.axis_size(axis_name) // 2
    pair = lax.axis_index(axis_name) // 2
    place = jnp.where(pair % 2 == 0, pair // 2, half - (pair + 1) // 2)

    def began(step):
        p = (place - step) % half
        return jnp.where(p < half // 2, 2 * p, 2 * (half - p) - 1)

    return began


def tile_of(extent, most):
    return max(t for t in range(128, most + 1, 128) if extent % t == 0)


def whole_block(shape):
    return pl.BlockSpec(shape, lambda *_: (0,) * len(shape))


def halves_spec(shape, tiles, second):
    if second:
        return pl.BlockSpec(shape, lambda i, *_: (jnp.maximum(i - tiles, 0), 0))
    return pl.BlockSpec(shape, lambda i, *_: (jnp.minimum(i, tiles - 1), 0))


def tile_index(i, tiles, at_ref):
    return jnp.where(i < tiles, at_ref[0], 1 - at_ref[0]) * tiles + i % tiles


def project_kernel(tiles, rows, at_ref, acts_ref, *refs):
    sums_ref = refs[-1]
    count = len(refs) // 2
    step = pl.program_id(0)
    lanes = refs[0].shape[1]

    @pl.when(step == 0)
    def _():
        sums_ref[...] = jnp.zeros_like(sums_ref)

    def add(pieces):
        total = sums_ref[...]
        for c in range(pieces[0].shape[0] // rows):
            part = jnp.concatenate([piece[c * rows : (c + 1) * rows] for piece in pieces], axis=0)
            total += lax.dot_general(
                part,
                acts_ref[:, c * lanes : (c + 1) * lanes],
                (((1,), (1,)), ((), ())),
                preferred_element_type=F32,
            )
        sums_ref[...] = total

    pl.when(step < tiles)(lambda: add(refs[:count]))
    pl.when(step >= tiles)(lambda: add(refs[count:-1]))


def project(owns, others, rows, core, acts, costed=False):
    tokens, units = acts.shape
    lanes = owns[0].shape[1]
    chunks = units // 2 // lanes
    if rows % 16:
        total = 0
        for pieces, side in ((owns, core), (others, 1 - core)):
            half = lax.dynamic_slice(acts, (0, side * (units // 2)), (tokens, units // 2))
            plain = [unchunk(piece, rows, chunks) for piece in pieces]
            total += jnp.concatenate(
                [lax.dot_general(p, half, (((1,), (1,)), ((), ())), preferred_element_type=F32) for p in plain]
            )
        return total
    group = max(g for g in range(1, chunks + 1) if chunks % g == 0 and g * lanes <= 4096)
    tiles = chunks // group
    return pl.pallas_call(
        functools.partial(project_kernel, tiles, rows),
        grid_spec=pltpu.PrefetchScalarGridSpec(
            num_scalar_prefetch=1,
            grid=(2 * tiles,),
            in_specs=[pl.BlockSpec((tokens, group * lanes), lambda i, at_ref: (0, tile_index(i, tiles, at_ref)))]
            + [halves_spec((group * rows, lanes), tiles, False)] * len(owns)
            + [halves_spec((group * rows, lanes), tiles, True)] * len(owns),
            out_specs=whole_block((len(owns) * rows, tokens)),
        ),
        out_shape=jax.ShapeDtypeStruct((len(owns) * rows, tokens), F32),
        compiler_params=pltpu.CompilerParams(vmem_limit_bytes=VMEM_BYTES),
        cost_estimate=pl.CostEstimate(
            flops=2 * len(owns) * rows * units * tokens if costed else 1,
            bytes_accessed=2 * units * (len(owns) * rows + tokens) if costed else 1,
            transcendentals=0,
        ),
        name="project_acts",
    )(core.astype(jnp.int32).reshape((1,)), acts, *owns, *others)


def unchunk(piece, rows, chunks):
    lanes = piece.shape[1]
    return piece[: chunks * rows].reshape((chunks, rows, lanes)).transpose(1, 0, 2).reshape((rows, -1))


def add_grads_kernel(at_ref, *refs):
    total_ref, out_ref, held, arrived = refs[-4:]
    count = (len(refs) - 4) // 2
    copies = []
    for k in range(count):
        start = refs[k].shape[0] - held.shape[1]
        copies.append(
            pltpu.make_async_copy(refs[k].at[pl.ds(start, held.shape[1])], held.at[k], arrived.at[k])
        )
        copies[-1].start()
    total = total_ref[...]
    for k in range(count):
        copies[k].wait()
        total += lax.dot_general(
            held[k], refs[count + k][0], (((1,), (1,)), ((), ())), preferred_element_type=F32
        )
    out_ref[...] = total


def add_grads(pieces, origins, wide_grads, total, n_dp):
    directions, units = total.shape[0], pieces[0].shape[1]
    n_mp, tokens, _ = wide_grads.shape
    share = n_dp // n_mp
    count = len(pieces)
    at = jnp.stack([f(origin, share) for origin in origins for f in (jnp.floor_divide, jnp.remainder)])

    def columns(k):
        return pl.BlockSpec((1, tokens, units), lambda i, at_ref: (at_ref[2 * k], 0, at_ref[2 * k + 1]))

    return pl.pallas_call(
        add_grads_kernel,
        grid_spec=pltpu.PrefetchScalarGridSpec(
            num_scalar_prefetch=1,
            grid=(1,),
            in_specs=[pl.BlockSpec(memory_space=pl.ANY)] * count
            + [columns(k) for k in range(count)]
            + [whole_block(total.shape)],
            out_specs=whole_block(total.shape),
            scratch_shapes=[
                pltpu.VMEM((count, directions, units), BF16),
                pltpu.SemaphoreType.DMA((count,)),
            ],
        ),
        out_shape=jax.ShapeDtypeStruct(total.shape, F32),
        compiler_params=pltpu.CompilerParams(vmem_limit_bytes=VMEM_BYTES),
        cost_estimate=pl.CostEstimate(flops=1, bytes_accessed=1, transcendentals=0),
        name="add_grads",
    )(at.astype(jnp.int32), *pieces, *[wide_grads] * count, total)


def join_kernel(at_ref, early_ref, late_ref, out_ref):
    count = early_ref.shape[0]
    for k in range(count):
        out_ref[at_ref[k]] = early_ref[k]
    out_ref[at_ref[count]] = late_ref[0]


def join(early, late, at):
    whole = pl.BlockSpec(memory_space=pltpu.VMEM)
    return pl.pallas_call(
        join_kernel,
        in_specs=[pl.BlockSpec(memory_space=pltpu.SMEM), whole, whole],
        out_specs=whole,
        out_shape=jax.ShapeDtypeStruct((early.shape[0] + 1,) + early.shape[1:], early.dtype),
        name="join_pairs",
    )(at, early, late)


def expand_kernel(tiles, rows, at_ref, near_ref, far_ref, turn_ref, *refs):
    out_ref, back, held = refs[-3:]
    count = back.shape[0] // rows
    step = pl.program_id(0)

    @pl.when(step == 0)
    def _():
        dims = (((0,), (0,)), ((), ()))
        depth = near_ref.shape[0]
        total = lax.dot_general(near_ref[...], turn_ref[:depth], dims, preferred_element_type=F32)
        total += lax.dot_general(far_ref[...], turn_ref[depth:], dims, preferred_element_type=F32)
        back[...] = total.astype(BF16)
        for k in range(count):
            start = pl.multiple_of(at_ref[1 + k] * rows, 16)
            held[k * rows : (k + 1) * rows] = back[pl.ds(start, rows)]

    def fill(pieces):
        lanes = pieces[0].shape[1]
        for c in range(pieces[0].shape[0] // rows):
            part = jnp.concatenate([piece[c * rows : (c + 1) * rows] for piece in pieces], axis=0)
            out_ref[c * lanes : (c + 1) * lanes] = lax.dot_general(
                part, held[...], (((0,), (0,)), ((), ())), preferred_element_type=F32
            ).astype(out_ref.dtype)

    pl.when(step < tiles)(lambda: fill(refs[:count]))
    pl.when(step >= tiles)(lambda: fill(refs[count:-3]))


def expand(owns, others, pairs, rows, units, core, near, far, turn):
    lanes = owns[0].shape[1]
    chunks = units // 2 // lanes
    columns = turn.shape[1]
    at = jnp.stack([core] + list(pairs)).astype(jnp.int32)
    if rows % 16:
        wide = jnp.concatenate([near, far])
        back = lax.dot_general(wide, turn, (((0,), (0,)), ((), ())), preferred_element_type=F32).astype(BF16)
        held = jnp.take(back.reshape((-1, rows, columns)), at[1:], axis=0).reshape((-1, columns))
        sides = []
        for pieces in (owns, others):
            plain = jnp.concatenate([unchunk(piece, rows, chunks) for piece in pieces])
            sides.append(lax.dot_general(plain, held, (((0,), (0,)), ((), ())), preferred_element_type=F32).astype(BF16))
        return jnp.where(core == 0, jnp.concatenate(sides), jnp.concatenate(sides[::-1]))
    group = max(g for g in range(1, chunks + 1) if chunks % g == 0 and g * lanes <= EXPAND_ROWS)
    tiles = chunks // group
    return pl.pallas_call(
        functools.partial(expand_kernel, tiles, rows),
        grid_spec=pltpu.PrefetchScalarGridSpec(
            num_scalar_prefetch=1,
            grid=(2 * tiles,),
            in_specs=[whole_block(near.shape), whole_block(far.shape), whole_block(turn.shape)]
            + [halves_spec((group * rows, lanes), tiles, False)] * len(owns)
            + [halves_spec((group * rows, lanes), tiles, True)] * len(owns),
            out_specs=pl.BlockSpec((group * lanes, columns), lambda i, at_ref: (tile_index(i, tiles, at_ref), 0)),
            scratch_shapes=[pltpu.VMEM((len(owns) * rows, columns), BF16)] * 2,
        ),
        out_shape=jax.ShapeDtypeStruct((units, columns), BF16),
        compiler_params=pltpu.CompilerParams(vmem_limit_bytes=VMEM_BYTES),
        cost_estimate=pl.CostEstimate(
            flops=2 * rows * len(owns) * units * columns, bytes_accessed=2 * units * columns, transcendentals=0
        ),
        name="expand_update",
    )(at, near, far, turn, *owns, *others)


def gather_near_first(x, axis_name):
    x = x[None]
    for bit in bits(axis_name):
        x = jnp.concatenate([x, flip(x, axis_name, bit)], axis=0)
    return x


def near_first(x, axis, me):
    size = x.shape[axis]
    for k in range(size.bit_length() - 1):
        shape = x.shape[:axis] + (size >> (k + 1), 2, 1 << k) + x.shape[axis + 1 :]
        parts = x.reshape(shape)
        swapped = jnp.flip(parts, axis + 1)
        x = jnp.where((me >> k) % 2 == 1, swapped, parts).reshape(x.shape)
    return x


def products(g, a):
    dims = (((1,), (1,)), ((), ()))
    g = g.astype(BF16)
    g_sq = (g.astype(F32) ** 2).astype(BF16)
    a_sq = (a.astype(F32) ** 2).astype(BF16)
    return (
        lax.dot_general(g, a, dims, preferred_element_type=F32),
        lax.dot_general(g_sq, a_sq, dims, preferred_element_type=F32),
    )


def picked(me_ref, g_ref, flipped):
    pairs = g_ref.shape[0] // 2
    core, pair = me_ref[0] % 2, me_ref[0] // 2
    return jnp.concatenate(
        [g_ref[(pair ^ r) * 2 + (core ^ flipped)] for r in range(pairs)], axis=0
    )


def theirs_kernel(rows, me_ref, at_ref, g_ref, *refs):
    out_ref, a_ref = refs[-2:]
    count = len(refs) // 2 - 1
    k = 0
    for own_ref, got_ref in zip(refs[:count], refs[count:-2]):
        total = (own_ref[...] + got_ref[...].astype(F32)).astype(BF16)
        for i in range(total.shape[0] // rows):
            start = pl.multiple_of(at_ref[k] * rows, 16)
            a_ref[pl.ds(start, rows)] = total[i * rows : (i + 1) * rows]
            k += 1
    rotated, squares = products(picked(me_ref, g_ref, 1), a_ref[...])
    out_ref[0] = rotated.astype(BF16)
    out_ref[1] = squares.astype(BF16)


def ours_kernel(me_ref, g_ref, a_ref, got_ref, *out_refs):
    width = g_ref.shape[1]
    rotated, squares = products(picked(me_ref, g_ref, 0), a_ref[...])
    rotated += got_ref[0].astype(F32)
    squares += got_ref[1].astype(F32)
    for r, out_ref in enumerate(out_refs):
        out_ref[0] = rotated[r * width : (r + 1) * width].astype(BF16)
        out_ref[1] = squares[r * width : (r + 1) * width].astype(BF16)


def token_sums(grad_proj_t, sums, gots, order, pair_rows):
    blocks, width, tokens = grad_proj_t.shape
    pairs = blocks // 2
    rows = pairs * pair_rows
    order = jnp.stack(order).astype(jnp.int32)
    me = lax.axis_index("dp")
    whole = pl.BlockSpec(memory_space=pltpu.VMEM)
    if width % 16 == 0 and pair_rows % 16 == 0 and gots:
        params = pltpu.CompilerParams(vmem_limit_bytes=VMEM_BYTES)
        cost = pl.CostEstimate(
            flops=2 * blocks * width * rows * tokens,
            bytes_accessed=4 * blocks * width * tokens + 2 * rows * tokens + 2 * blocks * width * rows,
            transcendentals=0,
        )
        index = me.astype(jnp.int32).reshape((1,))
        index_spec = pl.BlockSpec(memory_space=pltpu.SMEM)
        sent, act_proj_t = pl.pallas_call(
            functools.partial(theirs_kernel, pair_rows),
            in_specs=[index_spec, index_spec, whole] + [whole] * (len(sums) + len(gots)),
            out_specs=[whole, whole],
            out_shape=[
                jax.ShapeDtypeStruct((2, pairs * width, rows), BF16),
                jax.ShapeDtypeStruct((rows, tokens), BF16),
            ],
            compiler_params=params,
            cost_estimate=cost,
            name="sums_for_other_core",
        )(index, order, grad_proj_t, *sums, *gots)
        got = flip(sent, "dp", 1)
        ours = pl.pallas_call(
            ours_kernel,
            in_specs=[index_spec, whole, whole, whole],
            out_specs=[whole] * pairs,
            out_shape=[jax.ShapeDtypeStruct((2, width, rows), BF16)] * pairs,
            compiler_params=params,
            cost_estimate=cost,
            name="sums_for_own_core",
        )(index, grad_proj_t, act_proj_t, got)
    else:
        act_proj_t = jnp.concatenate(sums)
        for bit in bits("mp"):
            act_proj_t = act_proj_t + flip(act_proj_t.astype(BF16), "mp", bit).astype(F32)
        act_proj_t = act_proj_t.astype(BF16).reshape((-1, pair_rows, tokens))
        act_proj_t = join(act_proj_t[:-1], act_proj_t[-1:], order).reshape((-1, tokens))
        near = near_first(near_first(grad_proj_t.reshape((pairs, 2, width, tokens)), 0, me // 2), 1, me % 2)
        near = near.transpose(1, 0, 2, 3).reshape((2 * pairs * width, tokens))
        both = jnp.stack(products(near, act_proj_t)).reshape((2, 2, pairs, width, rows))
        total = both[:, 0] + flip(both[:, 1].astype(BF16), "dp", 1).astype(F32)
        ours = [total[:, r].astype(BF16) for r in range(pairs)]
    total = ours[0].astype(F32)
    for r in range(1, pairs):
        total += flip(ours[r], "dp", 2 * r).astype(F32)
    return total[0], total[1]


def gather_scaled(scaled, diag):
    pairs, n_mp = lax.axis_size("dp") // 2, lax.axis_size("mp")
    x = jnp.stack([scaled] + [flip(scaled, "dp", 2 * r) for r in range(2, pairs, 2)])
    parts = {}
    for m in range(n_mp):
        for low in range(2):
            hops = []
            for i in range(2 * pairs):
                hops += [(i * n_mp + k, (i ^ (2 * low)) * n_mp + (k ^ m)) for k in range(n_mp)]
            parts[m, low] = lax.ppermute(x, ("dp", "mp"), hops) if m or low else x
    x = jnp.stack([jnp.stack([parts[m, 0], parts[m, 1]], axis=1) for m in range(n_mp)])
    x, diag = lax.optimization_barrier((x, diag))
    return x, flip(x, "dp", 1), diag


def place_diag(diag_t):
    n_dp, n_mp = lax.axis_size("dp"), lax.axis_size("mp")
    width, rows = diag_t.shape[0], diag_t.shape[1] // n_mp
    here, block = lax.axis_index("mp"), lax.axis_index("mp") * n_dp + lax.axis_index("dp")
    out = jnp.zeros((n_mp, width, rows), diag_t.dtype)
    for k in range(n_mp):
        pairs = []
        for b in range(n_mp * n_dp):
            pairs.append(((b % n_dp) * n_mp + b // n_dp, (b // n_mp) * n_mp + (b + k) % n_mp))
        target = (block + k) % n_mp
        sent = lax.dynamic_slice(diag_t, (0, target * rows), (width, rows))
        got = lax.ppermute(sent, ("dp", "mp"), pairs)
        out = lax.dynamic_update_slice(out, got[None], ((here - k) % n_mp, 0, 0))
    return out.reshape((n_mp * width, rows)).T


def on_device(acts, grads, basis_in, basis_out, damping):
    tok_rows = acts.shape[0]
    n_dp, n_mp = lax.axis_size("dp"), lax.axis_size("mp")
    me = lax.axis_index("dp")
    tokens_all = tok_rows * n_dp
    out_units, directions = basis_out.shape
    width = directions // n_dp

    core, half = me % 2, n_dp // 2
    units = acts.shape[1]
    chunks = units // 2 // out_units
    own_rows = basis_in.shape[1]
    mine = basis_in.T.reshape((own_rows, 2, chunks, out_units)).transpose(1, 2, 0, 3)
    kept = lax.dynamic_index_in_dim(mine, core, 0, False)
    got = flip(lax.dynamic_index_in_dim(mine, 1 - core, 0, False), "dp", 1)
    both = jnp.stack([jnp.where(core == 0, kept, got), jnp.where(core == 0, got, kept)], axis=1)
    rows = 2 * own_rows
    in_rows = chunks * rows
    basis_out_t = basis_out.T
    own_piece = jnp.concatenate([both.reshape((in_rows, out_units)), basis_out_t])

    wide_grads = gather_doubling(grads, "mp")

    ahead, back_hops = ring_hops(n_dp)
    everyone = (ahead[0] + ahead[1], back_hops[0] + back_hops[1])
    last_hops = ahead[0] + back_hops[1]
    began = ring_place("dp")
    grad_proj_t = jnp.zeros((directions, tok_rows), F32)
    owns, others, pairs, sums, gots = [], [], [], [], []
    rows_near = basis_out_t

    def take_grads(pieces, where_from):
        nonlocal grad_proj_t
        origins = [2 * p + core for p in where_from] + [2 * p + 1 - core for p in where_from]
        grad_proj_t = add_grads(pieces, origins, wide_grads, grad_proj_t, n_dp)

    def use(pieces, where_from, grads_too=True, costed=False):
        swapped = [flip(piece, "dp", 1) for piece in pieces]
        sums.append(project(pieces, swapped, rows, core, acts, costed))
        gots.append([flip(sums[-1].astype(BF16), "mp", 1)] if n_mp == 2 else [])
        owns.extend(pieces)
        others.extend(swapped)
        pairs.extend(where_from)
        if grads_too:
            take_grads(pieces + swapped, where_from)

    moving = [own_piece, own_piece]
    waiting = [own_piece], [me // 2]
    for step in range(1, half // 2):
        moving = [lax.ppermute(x, "dp", everyone[k]) for k, x in enumerate(moving)]
        if step == 1:
            moving, own_piece = lax.optimization_barrier((moving, own_piece))
            waiting = [own_piece], [me // 2]
        else:
            use(*waiting)
            moving, sums[-1], gots[:-1], grad_proj_t, rows_near = lax.optimization_barrier(
                (moving, sums[-1], gots[:-1], grad_proj_t, rows_near)
            )
            waiting = [], []
        if step == min(2, half // 2 - 1):
            rows_near = gather_near_first(rows_near, "mp")
        waiting = waiting[0] + moving, waiting[1] + [began(step), began(-step)]

    last = lax.ppermute(
        jnp.where(core == 0, moving[0][:in_rows], moving[1][:in_rows]), "dp", last_hops
    )
    held = jnp.where(core == 0, moving[0][in_rows:], moving[1][in_rows:])
    use(*waiting)
    held, last, sums[-1], grad_proj_t = lax.optimization_barrier((held, last, sums[-1], grad_proj_t))
    last_out = lax.ppermute(held, "dp", last_hops)
    last_pair = began(half // 2)
    use([last], [last_pair], False, True)
    last_out, sums[-1] = lax.optimization_barrier((last_out, sums[-1]))
    grad_proj_t = add_grads(
        [last_out, flip(last_out, "dp", 1)],
        [2 * last_pair + core, 2 * last_pair + 1 - core],
        wide_grads,
        grad_proj_t,
        n_dp,
    )

    rows_near = rows_near.reshape((n_mp, half, 2, width, out_units))
    rows_near = near_first(near_first(rows_near, 1, me // 2), 2, core)
    rows_near = rows_near.transpose(2, 0, 1, 3, 4).reshape((n_mp * directions, out_units))

    rotated, squares = token_sums(
        grad_proj_t.reshape((n_dp, width, tok_rows)), sums, [got for part in gots for got in part], pairs, rows
    )
    diag_t = squares / tokens_all
    scaled = (rotated / (diag_t + damping[0])).astype(BF16)
    near, far, diag = gather_scaled(scaled, place_diag(diag_t))
    near, far = (x.reshape((directions * n_mp // 2, -1)) for x in (near, far))
    return (expand(owns, others, pairs, rows, units, core, near, far, rows_near), diag)


def solution(mesh):
    placed = (P("dp", "mp"), P("dp", "mp"), P("mp", "dp"), P("dp", "mp"), P())
    return jax.shard_map(
        on_device,
        mesh=mesh,
        in_specs=placed,
        out_specs=(P("mp", "dp"), P("mp", "dp")),
        check_vma=False,
    )
```

```python
import functools

import jax
import jax.numpy as jnp
from jax import lax
from jax.experimental import pallas as pl
from jax.experimental.pallas import tpu as pltpu
from jax.sharding import PartitionSpec as P

BF16, F32 = jnp.bfloat16, jnp.float32
VMEM_BYTES = 48 * 1024 * 1024
EXPAND_ROWS = 4096
AHEAD = 2
PROJECT_UNITS = 8192


def flip(x, axis_name, bit):
    size = lax.axis_size(axis_name)
    return lax.ppermute(x, axis_name, [(i, i ^ bit) for i in range(size)])


def bits(axis_name):
    size = lax.axis_size(axis_name)
    assert size & (size - 1) == 0
    return [1 << k for k in range(size.bit_length() - 1)]


def gather_doubling(x, axis_name):
    me = lax.axis_index(axis_name)
    x = x[None]
    for bit in reversed(bits(axis_name)):
        other = flip(x, axis_name, bit)
        side = (me // bit) % 2
        low = jnp.where(side == 0, x, other)
        high = jnp.where(side == 0, other, x)
        x = jnp.stack([low, high], axis=1).reshape((2 * x.shape[0],) + x.shape[1:])
    return x


def ring_hops(size):
    half = size // 2
    order = list(range(0, half, 2)) + list(range(half - 1, 0, -2))
    hops = [(order[k], order[(k + 1) % half]) for k in range(half)]
    ahead = [[(2 * s + c, 2 * d + c) for s, d in hops] for c in (0, 1)]
    return ahead, [[(d, s) for s, d in part] for part in ahead]


def ring_place(axis_name):
    half = lax.axis_size(axis_name) // 2
    pair = lax.axis_index(axis_name) // 2
    place = jnp.where(pair % 2 == 0, pair // 2, half - (pair + 1) // 2)

    def began(step):
        p = (place - step) % half
        return jnp.where(p < half // 2, 2 * p, 2 * (half - p) - 1)

    return began


def tile_of(extent, most):
    return max(t for t in range(128, most + 1, 128) if extent % t == 0)


def whole_block(shape):
    return pl.BlockSpec(shape, lambda *_: (0,) * len(shape))


def halves_spec(shape, tiles, second):
    if second:
        return pl.BlockSpec(shape, lambda i, *_: (jnp.maximum(i - tiles, 0), 0))
    return pl.BlockSpec(shape, lambda i, *_: (jnp.minimum(i, tiles - 1), 0))


def tile_index(i, tiles, at_ref):
    return jnp.where(i < tiles, at_ref[0], 1 - at_ref[0]) * tiles + i % tiles


def project_kernel(tiles, rows, at_ref, acts_ref, *refs):
    sums_ref, held = refs[-2:]
    count = len(refs) // 2 - 1
    step = pl.program_id(0)
    lanes = refs[0].shape[1]

    @pl.when(step == 0)
    def _():
        held[...] = jnp.zeros_like(held)

    def add(pieces):
        total = held[...]
        for c in range(pieces[0].shape[0] // rows):
            part = jnp.concatenate([piece[c * rows : (c + 1) * rows] for piece in pieces], axis=0)
            total += lax.dot_general(
                acts_ref[:, c * lanes : (c + 1) * lanes],
                part,
                (((1,), (1,)), ((), ())),
                preferred_element_type=F32,
            )
        held[...] = total

    pl.when(step < tiles)(lambda: add(refs[:count]))
    pl.when(step >= tiles)(lambda: add(refs[count:-2]))

    @pl.when(step == 2 * tiles - 1)
    def _():
        sums_ref[...] = held[...].T


def project(owns, others, rows, core, acts, costed=False):
    tokens, units = acts.shape
    lanes = owns[0].shape[1]
    chunks = units // 2 // lanes
    if rows % 16:
        total = 0
        for pieces, side in ((owns, core), (others, 1 - core)):
            half = lax.dynamic_slice(acts, (0, side * (units // 2)), (tokens, units // 2))
            plain = [unchunk(piece, rows, chunks) for piece in pieces]
            total += jnp.concatenate(
                [lax.dot_general(p, half, (((1,), (1,)), ((), ())), preferred_element_type=F32) for p in plain]
            )
        return total
    group = max(g for g in range(1, chunks + 1) if chunks % g == 0 and g * lanes <= PROJECT_UNITS)
    tiles = chunks // group
    return pl.pallas_call(
        functools.partial(project_kernel, tiles, rows),
        grid_spec=pltpu.PrefetchScalarGridSpec(
            num_scalar_prefetch=1,
            grid=(2 * tiles,),
            in_specs=[pl.BlockSpec((tokens, group * lanes), lambda i, at_ref: (0, tile_index(i, tiles, at_ref)))]
            + [halves_spec((group * rows, lanes), tiles, False)] * len(owns)
            + [halves_spec((group * rows, lanes), tiles, True)] * len(owns),
            out_specs=whole_block((len(owns) * rows, tokens)),
            scratch_shapes=[pltpu.VMEM((tokens, len(owns) * rows), F32)],
        ),
        out_shape=jax.ShapeDtypeStruct((len(owns) * rows, tokens), F32),
        compiler_params=pltpu.CompilerParams(vmem_limit_bytes=VMEM_BYTES),
        cost_estimate=pl.CostEstimate(
            flops=2 * len(owns) * rows * units * tokens if costed else 1,
            bytes_accessed=2 * units * (len(owns) * rows + tokens) if costed else 1,
            transcendentals=0,
        ),
        name="project_acts",
    )(core.astype(jnp.int32).reshape((1,)), acts, *owns, *others)


def unchunk(piece, rows, chunks):
    lanes = piece.shape[1]
    return piece[: chunks * rows].reshape((chunks, rows, lanes)).transpose(1, 0, 2).reshape((rows, -1))


def add_grads_kernel(at_ref, *refs):
    total_ref, out_ref, held, arrived = refs[-4:]
    count = (len(refs) - 4) // 2
    copies = []
    for k in range(count):
        start = refs[k].shape[0] - held.shape[1]
        copies.append(
            pltpu.make_async_copy(refs[k].at[pl.ds(start, held.shape[1])], held.at[k], arrived.at[k])
        )
        copies[-1].start()
    total = total_ref[...]
    for k in range(count):
        copies[k].wait()
        total += lax.dot_general(
            held[k], refs[count + k][0], (((1,), (1,)), ((), ())), preferred_element_type=F32
        )
    out_ref[...] = total


def add_grads(pieces, origins, wide_grads, total, n_dp):
    directions, units = total.shape[0], pieces[0].shape[1]
    n_mp, tokens, _ = wide_grads.shape
    share = n_dp // n_mp
    count = len(pieces)
    at = jnp.stack([f(origin, share) for origin in origins for f in (jnp.floor_divide, jnp.remainder)])

    def columns(k):
        return pl.BlockSpec((1, tokens, units), lambda i, at_ref: (at_ref[2 * k], 0, at_ref[2 * k + 1]))

    return pl.pallas_call(
        add_grads_kernel,
        grid_spec=pltpu.PrefetchScalarGridSpec(
            num_scalar_prefetch=1,
            grid=(1,),
            in_specs=[pl.BlockSpec(memory_space=pl.ANY)] * count
            + [columns(k) for k in range(count)]
            + [whole_block(total.shape)],
            out_specs=whole_block(total.shape),
            scratch_shapes=[
                pltpu.VMEM((count, directions, units), BF16),
                pltpu.SemaphoreType.DMA((count,)),
            ],
        ),
        out_shape=jax.ShapeDtypeStruct(total.shape, F32),
        compiler_params=pltpu.CompilerParams(vmem_limit_bytes=VMEM_BYTES),
        cost_estimate=pl.CostEstimate(flops=1, bytes_accessed=1, transcendentals=0),
        name="add_grads",
    )(at.astype(jnp.int32), *pieces, *[wide_grads] * count, total)


def join_kernel(at_ref, early_ref, late_ref, out_ref):
    count = early_ref.shape[0]
    for k in range(count):
        out_ref[at_ref[k]] = early_ref[k]
    out_ref[at_ref[count]] = late_ref[0]


def join(early, late, at):
    whole = pl.BlockSpec(memory_space=pltpu.VMEM)
    return pl.pallas_call(
        join_kernel,
        in_specs=[pl.BlockSpec(memory_space=pltpu.SMEM), whole, whole],
        out_specs=whole,
        out_shape=jax.ShapeDtypeStruct((early.shape[0] + 1,) + early.shape[1:], early.dtype),
        name="join_pairs",
    )(at, early, late)


def expand_kernel(tiles, rows, at_ref, near_ref, far_ref, turn_ref, *refs):
    count = (len(refs) - 9) // 2
    owns, others, out_ref = refs[:count], refs[count : 2 * count], refs[2 * count]
    scaled, turned, back, held, pieces, sent, first_sem, piece_sem, out_sem = refs[-9:]
    deep = pieces.shape[2]
    ahead = min(AHEAD, tiles)
    depth, lanes = near_ref.shape[0], pieces.shape[3]
    out_rows = sent.shape[1]

    def fetch(group, half, t):
        tile = half * tiles + t
        return [
            pltpu.make_async_copy(ref.at[pl.ds(t * deep, deep)], pieces.at[tile, k], piece_sem.at[tile, k])
            for k, ref in enumerate(group)
        ]

    def store(half, t):
        side = at_ref[0] if half == 0 else 1 - at_ref[0]
        tile = half * tiles + t
        return pltpu.make_async_copy(
            sent.at[tile % 2], out_ref.at[pl.ds((side * tiles + t) * out_rows, out_rows)], out_sem.at[tile % 2]
        )

    opening = [
        pltpu.make_async_copy(near_ref, scaled.at[0], first_sem.at[0]),
        pltpu.make_async_copy(far_ref, scaled.at[1], first_sem.at[1]),
        pltpu.make_async_copy(turn_ref, turned, first_sem.at[2]),
    ]
    for copy in opening:
        copy.start()
    for t in range(ahead):
        for copy in fetch(owns, 0, t):
            copy.start()
    for copy in opening:
        copy.wait()
    dims = (((0,), (0,)), ((), ()))
    total = lax.dot_general(scaled[0], turned[:depth], dims, preferred_element_type=F32)
    total += lax.dot_general(scaled[1], turned[depth:], dims, preferred_element_type=F32)
    back[...] = total.astype(BF16)
    for k in range(count):
        start = pl.multiple_of(at_ref[1 + k] * rows, 16)
        held[k * rows : (k + 1) * rows] = back[pl.ds(start, rows)]

    def step(half, group, t, more, next_half, next_group, next_t, settled):
        if more:
            for copy in fetch(next_group, next_half, next_t):
                copy.start()
        for copy in fetch(group, half, t):
            copy.wait()
        tile = half * tiles + t
        if settled is not None:
            store(*settled).wait()
        for c in range(deep // rows):
            part = jnp.concatenate([pieces[tile, k, c * rows : (c + 1) * rows] for k in range(count)], axis=0)
            sent[tile % 2, c * lanes : (c + 1) * lanes] = lax.dot_general(
                part, held[...], dims, preferred_element_type=F32
            ).astype(BF16)
        store(half, t).start()

    for half, group in ((0, owns), (1, others)):
        for t in range(tiles):
            tile = half * tiles + t
            coming = tile + ahead
            before = tile - 2
            step(
                half,
                group,
                t,
                coming < 2 * tiles,
                coming // tiles,
                owns if coming < tiles else others,
                coming % tiles,
                (before // tiles, before % tiles) if before >= 0 else None,
            )
    for tile in (2 * tiles - 2, 2 * tiles - 1):
        store(tile // tiles, tile % tiles).wait()


def expand(owns, others, pairs, rows, units, core, near, far, turn):
    lanes = owns[0].shape[1]
    chunks = units // 2 // lanes
    columns = turn.shape[1]
    at = jnp.stack([core] + list(pairs)).astype(jnp.int32)
    if rows % 16:
        wide = jnp.concatenate([near, far])
        back = lax.dot_general(wide, turn, (((0,), (0,)), ((), ())), preferred_element_type=F32).astype(BF16)
        held = jnp.take(back.reshape((-1, rows, columns)), at[1:], axis=0).reshape((-1, columns))
        sides = []
        for pieces in (owns, others):
            plain = jnp.concatenate([unchunk(piece, rows, chunks) for piece in pieces])
            sides.append(lax.dot_general(plain, held, (((0,), (0,)), ((), ())), preferred_element_type=F32).astype(BF16))
        return jnp.where(core == 0, jnp.concatenate(sides), jnp.concatenate(sides[::-1]))
    group = max(g for g in range(1, chunks + 1) if chunks % g == 0 and g * lanes <= EXPAND_ROWS)
    tiles = chunks // group
    count = len(owns)
    anywhere = pl.BlockSpec(memory_space=pl.ANY)
    return pl.pallas_call(
        functools.partial(expand_kernel, tiles, rows),
        grid_spec=pltpu.PrefetchScalarGridSpec(
            num_scalar_prefetch=1,
            grid=(1,),
            in_specs=[anywhere] * (3 + 2 * count),
            out_specs=anywhere,
            scratch_shapes=[
                pltpu.VMEM((2,) + near.shape, BF16),
                pltpu.VMEM(turn.shape, BF16),
                pltpu.VMEM((count * rows, columns), BF16),
                pltpu.VMEM((count * rows, columns), BF16),
                pltpu.VMEM((2 * tiles, count, group * rows, lanes), BF16),
                pltpu.VMEM((2, group * lanes, columns), BF16),
                pltpu.SemaphoreType.DMA((3,)),
                pltpu.SemaphoreType.DMA((2 * tiles, count)),
                pltpu.SemaphoreType.DMA((2,)),
            ],
        ),
        out_shape=jax.ShapeDtypeStruct((units, columns), BF16),
        compiler_params=pltpu.CompilerParams(vmem_limit_bytes=VMEM_BYTES),
        cost_estimate=pl.CostEstimate(
            flops=2 * rows * count * units * columns, bytes_accessed=2 * units * columns, transcendentals=0
        ),
        name="expand_update",
    )(at, near, far, turn, *owns, *others)


def gather_near_first(x, axis_name):
    x = x[None]
    for bit in bits(axis_name):
        x = jnp.concatenate([x, flip(x, axis_name, bit)], axis=0)
    return x


def near_first(x, axis, me):
    size = x.shape[axis]
    for k in range(size.bit_length() - 1):
        shape = x.shape[:axis] + (size >> (k + 1), 2, 1 << k) + x.shape[axis + 1 :]
        parts = x.reshape(shape)
        swapped = jnp.flip(parts, axis + 1)
        x = jnp.where((me >> k) % 2 == 1, swapped, parts).reshape(x.shape)
    return x


def products(g, a):
    dims = (((1,), (1,)), ((), ()))
    g = g.astype(BF16)
    g_sq = (g.astype(F32) ** 2).astype(BF16)
    a_sq = (a.astype(F32) ** 2).astype(BF16)
    return (
        lax.dot_general(g, a, dims, preferred_element_type=F32),
        lax.dot_general(g_sq, a_sq, dims, preferred_element_type=F32),
    )


def picked(me_ref, g_ref, flipped):
    pairs = g_ref.shape[0] // 2
    core, pair = me_ref[0] % 2, me_ref[0] // 2
    return jnp.concatenate(
        [g_ref[(pair ^ r) * 2 + (core ^ flipped)] for r in range(pairs)], axis=0
    )


def theirs_kernel(rows, me_ref, at_ref, g_ref, *refs):
    out_ref, a_ref = refs[-2:]
    count = len(refs) // 2 - 1
    k = 0
    for own_ref, got_ref in zip(refs[:count], refs[count:-2]):
        total = (own_ref[...] + got_ref[...].astype(F32)).astype(BF16)
        for i in range(total.shape[0] // rows):
            start = pl.multiple_of(at_ref[k] * rows, 16)
            a_ref[pl.ds(start, rows)] = total[i * rows : (i + 1) * rows]
            k += 1
    rotated, squares = products(picked(me_ref, g_ref, 1), a_ref[...])
    out_ref[0] = rotated.astype(BF16)
    out_ref[1] = squares.astype(BF16)


def ours_kernel(me_ref, g_ref, a_ref, got_ref, *out_refs):
    width = g_ref.shape[1]
    rotated, squares = products(picked(me_ref, g_ref, 0), a_ref[...])
    rotated += got_ref[0].astype(F32)
    squares += got_ref[1].astype(F32)
    for r, out_ref in enumerate(out_refs):
        out_ref[0] = rotated[r * width : (r + 1) * width].astype(BF16)
        out_ref[1] = squares[r * width : (r + 1) * width].astype(BF16)


def token_sums(grad_proj_t, sums, gots, order, pair_rows):
    blocks, width, tokens = grad_proj_t.shape
    pairs = blocks // 2
    rows = pairs * pair_rows
    order = jnp.stack(order).astype(jnp.int32)
    me = lax.axis_index("dp")
    whole = pl.BlockSpec(memory_space=pltpu.VMEM)
    if width % 16 == 0 and pair_rows % 16 == 0 and gots:
        params = pltpu.CompilerParams(vmem_limit_bytes=VMEM_BYTES)
        cost = pl.CostEstimate(
            flops=2 * blocks * width * rows * tokens,
            bytes_accessed=4 * blocks * width * tokens + 2 * rows * tokens + 2 * blocks * width * rows,
            transcendentals=0,
        )
        index = me.astype(jnp.int32).reshape((1,))
        index_spec = pl.BlockSpec(memory_space=pltpu.SMEM)
        sent, act_proj_t = pl.pallas_call(
            functools.partial(theirs_kernel, pair_rows),
            in_specs=[index_spec, index_spec, whole] + [whole] * (len(sums) + len(gots)),
            out_specs=[whole, whole],
            out_shape=[
                jax.ShapeDtypeStruct((2, pairs * width, rows), BF16),
                jax.ShapeDtypeStruct((rows, tokens), BF16),
            ],
            compiler_params=params,
            cost_estimate=cost,
            name="sums_for_other_core",
        )(index, order, grad_proj_t, *sums, *gots)
        got = flip(sent, "dp", 1)
        ours = pl.pallas_call(
            ours_kernel,
            in_specs=[index_spec, whole, whole, whole],
            out_specs=[whole] * pairs,
            out_shape=[jax.ShapeDtypeStruct((2, width, rows), BF16)] * pairs,
            compiler_params=params,
            cost_estimate=cost,
            name="sums_for_own_core",
        )(index, grad_proj_t, act_proj_t, got)
    else:
        act_proj_t = jnp.concatenate(sums)
        for bit in bits("mp"):
            act_proj_t = act_proj_t + flip(act_proj_t.astype(BF16), "mp", bit).astype(F32)
        act_proj_t = act_proj_t.astype(BF16).reshape((-1, pair_rows, tokens))
        act_proj_t = join(act_proj_t[:-1], act_proj_t[-1:], order).reshape((-1, tokens))
        near = near_first(near_first(grad_proj_t.reshape((pairs, 2, width, tokens)), 0, me // 2), 1, me % 2)
        near = near.transpose(1, 0, 2, 3).reshape((2 * pairs * width, tokens))
        both = jnp.stack(products(near, act_proj_t)).reshape((2, 2, pairs, width, rows))
        total = both[:, 0] + flip(both[:, 1].astype(BF16), "dp", 1).astype(F32)
        ours = [total[:, r].astype(BF16) for r in range(pairs)]
    total = ours[0].astype(F32)
    for r in range(1, pairs):
        total += flip(ours[r], "dp", 2 * r).astype(F32)
    return total[0], total[1]


def gather_scaled(scaled, diag):
    pairs, n_mp = lax.axis_size("dp") // 2, lax.axis_size("mp")
    x = jnp.stack([scaled] + [flip(scaled, "dp", 2 * r) for r in range(2, pairs, 2)])
    parts = {}
    for m in range(n_mp):
        for low in range(2):
            hops = []
            for i in range(2 * pairs):
                hops += [(i * n_mp + k, (i ^ (2 * low)) * n_mp + (k ^ m)) for k in range(n_mp)]
            parts[m, low] = lax.ppermute(x, ("dp", "mp"), hops) if m or low else x
    x = jnp.stack([jnp.stack([parts[m, 0], parts[m, 1]], axis=1) for m in range(n_mp)])
    x, diag = lax.optimization_barrier((x, diag))
    return x, flip(x, "dp", 1), diag


def place_diag(diag_t):
    n_dp, n_mp = lax.axis_size("dp"), lax.axis_size("mp")
    width, rows = diag_t.shape[0], diag_t.shape[1] // n_mp
    here, block = lax.axis_index("mp"), lax.axis_index("mp") * n_dp + lax.axis_index("dp")
    out = jnp.zeros((n_mp, width, rows), diag_t.dtype)
    for k in range(n_mp):
        pairs = []
        for b in range(n_mp * n_dp):
            pairs.append(((b % n_dp) * n_mp + b // n_dp, (b // n_mp) * n_mp + (b + k) % n_mp))
        target = (block + k) % n_mp
        sent = lax.dynamic_slice(diag_t, (0, target * rows), (width, rows))
        got = lax.ppermute(sent, ("dp", "mp"), pairs)
        out = lax.dynamic_update_slice(out, got[None], ((here - k) % n_mp, 0, 0))
    return out.reshape((n_mp * width, rows)).T


def on_device(acts, grads, basis_in, basis_out, damping):
    tok_rows = acts.shape[0]
    n_dp, n_mp = lax.axis_size("dp"), lax.axis_size("mp")
    me = lax.axis_index("dp")
    tokens_all = tok_rows * n_dp
    out_units, directions = basis_out.shape
    width = directions // n_dp

    core, half = me % 2, n_dp // 2
    units = acts.shape[1]
    chunks = units // 2 // out_units
    own_rows = basis_in.shape[1]
    mine = basis_in.T

    def side_of(side):
        part = lax.dynamic_slice(mine, (0, side * (units // 2)), (own_rows, units // 2))
        return jnp.stack([part[:, c * out_units : (c + 1) * out_units] for c in range(chunks)])

    kept = side_of(core)
    got = flip(side_of(1 - core), "dp", 1)
    both = jnp.stack([jnp.where(core == 0, kept, got), jnp.where(core == 0, got, kept)], axis=1)
    rows = 2 * own_rows
    in_rows = chunks * rows
    basis_out_t = basis_out.T
    own_piece = jnp.concatenate([both.reshape((in_rows, out_units)), basis_out_t])

    wide_grads = gather_doubling(grads, "mp")

    ahead, back_hops = ring_hops(n_dp)
    everyone = (ahead[0] + ahead[1], back_hops[0] + back_hops[1])
    last_hops = ahead[0] + back_hops[1]
    began = ring_place("dp")
    grad_proj_t = jnp.zeros((directions, tok_rows), F32)
    owns, others, pairs, sums, gots = [], [], [], [], []
    rows_near = basis_out_t

    def take_grads(pieces, where_from):
        nonlocal grad_proj_t
        origins = [2 * p + core for p in where_from] + [2 * p + 1 - core for p in where_from]
        grad_proj_t = add_grads(pieces, origins, wide_grads, grad_proj_t, n_dp)

    def use(pieces, where_from, grads_too=True, costed=False, known=()):
        swapped = list(known) + [flip(piece, "dp", 1) for piece in pieces[len(known) :]]
        sums.append(project(pieces, swapped, rows, core, acts, costed))
        gots.append([flip(sums[-1].astype(BF16), "mp", 1)] if n_mp == 2 else [])
        owns.extend(pieces)
        others.extend(swapped)
        pairs.extend(where_from)
        if grads_too:
            take_grads(pieces + swapped, where_from)

    moving = [own_piece, own_piece]
    waiting = [own_piece], [me // 2]
    for step in range(1, half // 2):
        moving = [lax.ppermute(x, "dp", everyone[k]) for k, x in enumerate(moving)]
        if step == 1:
            swapped = flip(own_piece, "dp", 1)
            moving, own_piece, swapped = lax.optimization_barrier((moving, own_piece, swapped))
            waiting = [own_piece], [me // 2]
        else:
            use(*waiting, known=[swapped] if step == 2 else [])
            moving, sums[-1], gots[:-1], grad_proj_t, rows_near = lax.optimization_barrier(
                (moving, sums[-1], gots[:-1], grad_proj_t, rows_near)
            )
            waiting = [], []
        if step == min(2, half // 2 - 1):
            rows_near = gather_near_first(rows_near, "mp")
        waiting = waiting[0] + moving, waiting[1] + [began(step), began(-step)]

    last = lax.ppermute(
        jnp.where(core == 0, moving[0][:in_rows], moving[1][:in_rows]), "dp", last_hops
    )
    held = jnp.where(core == 0, moving[0][in_rows:], moving[1][in_rows:])
    use(*waiting)
    held, last, sums[-1], gots[:-1], grad_proj_t = lax.optimization_barrier(
        (held, last, sums[-1], gots[:-1], grad_proj_t)
    )
    last_out = lax.ppermute(held, "dp", last_hops)
    last_pair = began(half // 2)
    use([last], [last_pair], False, True)
    last_out, sums[-1], gots[:-1] = lax.optimization_barrier((last_out, sums[-1], gots[:-1]))
    grad_proj_t = add_grads(
        [last_out, flip(last_out, "dp", 1)],
        [2 * last_pair + core, 2 * last_pair + 1 - core],
        wide_grads,
        grad_proj_t,
        n_dp,
    )

    rows_near = rows_near.reshape((n_mp, half, 2, width, out_units))
    rows_near = near_first(near_first(rows_near, 1, me // 2), 2, core)
    rows_near = rows_near.transpose(2, 0, 1, 3, 4).reshape((n_mp * directions, out_units))

    rotated, squares = token_sums(
        grad_proj_t.reshape((n_dp, width, tok_rows)), sums, [got for part in gots for got in part], pairs, rows
    )
    diag_t = squares / tokens_all
    scaled = (rotated / (diag_t + damping[0])).astype(BF16)
    near, far, diag = gather_scaled(scaled, place_diag(diag_t))
    near, far = (x.reshape((directions * n_mp // 2, -1)) for x in (near, far))
    return (expand(owns, others, pairs, rows, units, core, near, far, rows_near), diag)


def solution(mesh):
    placed = (P("dp", "mp"), P("dp", "mp"), P("mp", "dp"), P("dp", "mp"), P())
    return jax.shard_map(
        on_device,
        mesh=mesh,
        in_specs=placed,
        out_specs=(P("mp", "dp"), P("mp", "dp")),
        check_vma=False,
    )
```

```python
import functools

import jax
import jax.numpy as jnp
from jax import lax
from jax.experimental import pallas as pl
from jax.experimental.pallas import tpu as pltpu
from jax.sharding import PartitionSpec as P

BF16, F32 = jnp.bfloat16, jnp.float32
VMEM_BYTES = 48 * 1024 * 1024
EXPAND_ROWS = 4096
AHEAD = 2
PROJECT_UNITS = 8192


def flip(x, axis_name, bit):
    size = lax.axis_size(axis_name)
    return lax.ppermute(x, axis_name, [(i, i ^ bit) for i in range(size)])


def bits(axis_name):
    size = lax.axis_size(axis_name)
    assert size & (size - 1) == 0
    return [1 << k for k in range(size.bit_length() - 1)]


def gather_doubling(x, axis_name):
    me = lax.axis_index(axis_name)
    x = x[None]
    for bit in reversed(bits(axis_name)):
        other = flip(x, axis_name, bit)
        side = (me // bit) % 2
        low = jnp.where(side == 0, x, other)
        high = jnp.where(side == 0, other, x)
        x = jnp.stack([low, high], axis=1).reshape((2 * x.shape[0],) + x.shape[1:])
    return x


def ring_hops(size):
    half = size // 2
    order = list(range(0, half, 2)) + list(range(half - 1, 0, -2))
    hops = [(order[k], order[(k + 1) % half]) for k in range(half)]
    ahead = [[(2 * s + c, 2 * d + c) for s, d in hops] for c in (0, 1)]
    return ahead, [[(d, s) for s, d in part] for part in ahead]


def ring_place(axis_name):
    half = lax.axis_size(axis_name) // 2
    pair = lax.axis_index(axis_name) // 2
    place = jnp.where(pair % 2 == 0, pair // 2, half - (pair + 1) // 2)

    def began(step):
        p = (place - step) % half
        return jnp.where(p < half // 2, 2 * p, 2 * (half - p) - 1)

    return began


def tile_of(extent, most):
    return max(t for t in range(128, most + 1, 128) if extent % t == 0)


def whole_block(shape):
    return pl.BlockSpec(shape, lambda *_: (0,) * len(shape))


def halves_spec(shape, tiles, second):
    if second:
        return pl.BlockSpec(shape, lambda i, *_: (jnp.maximum(i - tiles, 0), 0))
    return pl.BlockSpec(shape, lambda i, *_: (jnp.minimum(i, tiles - 1), 0))


def tile_index(i, tiles, at_ref):
    return jnp.where(i < tiles, at_ref[0], 1 - at_ref[0]) * tiles + i % tiles


def project_kernel(tiles, rows, at_ref, acts_ref, *refs):
    sums_ref, held = refs[-2:]
    count = len(refs) // 2 - 1
    step = pl.program_id(0)
    lanes = refs[0].shape[1]

    @pl.when(step == 0)
    def _():
        held[...] = jnp.zeros_like(held)

    def add(pieces):
        total = held[...]
        for c in range(pieces[0].shape[0] // rows):
            part = jnp.concatenate([piece[c * rows : (c + 1) * rows] for piece in pieces], axis=0)
            total += lax.dot_general(
                acts_ref[:, c * lanes : (c + 1) * lanes],
                part,
                (((1,), (1,)), ((), ())),
                preferred_element_type=F32,
            )
        held[...] = total

    pl.when(step < tiles)(lambda: add(refs[:count]))
    pl.when(step >= tiles)(lambda: add(refs[count:-2]))

    @pl.when(step == 2 * tiles - 1)
    def _():
        sums_ref[...] = held[...].T


def project(owns, others, rows, core, acts, costed=False):
    tokens, units = acts.shape
    lanes = owns[0].shape[1]
    chunks = units // 2 // lanes
    if rows % 16:
        total = 0
        for pieces, side in ((owns, core), (others, 1 - core)):
            half = lax.dynamic_slice(acts, (0, side * (units // 2)), (tokens, units // 2))
            plain = [unchunk(piece, rows, chunks) for piece in pieces]
            total += jnp.concatenate(
                [lax.dot_general(p, half, (((1,), (1,)), ((), ())), preferred_element_type=F32) for p in plain]
            )
        return total
    group = max(g for g in range(1, chunks + 1) if chunks % g == 0 and g * lanes <= PROJECT_UNITS)
    tiles = chunks // group
    return pl.pallas_call(
        functools.partial(project_kernel, tiles, rows),
        grid_spec=pltpu.PrefetchScalarGridSpec(
            num_scalar_prefetch=1,
            grid=(2 * tiles,),
            in_specs=[pl.BlockSpec((tokens, group * lanes), lambda i, at_ref: (0, tile_index(i, tiles, at_ref)))]
            + [halves_spec((group * rows, lanes), tiles, False)] * len(owns)
            + [halves_spec((group * rows, lanes), tiles, True)] * len(owns),
            out_specs=whole_block((len(owns) * rows, tokens)),
            scratch_shapes=[pltpu.VMEM((tokens, len(owns) * rows), F32)],
        ),
        out_shape=jax.ShapeDtypeStruct((len(owns) * rows, tokens), F32),
        compiler_params=pltpu.CompilerParams(vmem_limit_bytes=VMEM_BYTES),
        cost_estimate=pl.CostEstimate(
            flops=2 * len(owns) * rows * units * tokens if costed else 1,
            bytes_accessed=2 * units * (len(owns) * rows + tokens) if costed else 1,
            transcendentals=0,
        ),
        name="project_acts",
    )(core.astype(jnp.int32).reshape((1,)), acts, *owns, *others)


def unchunk(piece, rows, chunks):
    lanes = piece.shape[1]
    return piece[: chunks * rows].reshape((chunks, rows, lanes)).transpose(1, 0, 2).reshape((rows, -1))


def add_grads_kernel(at_ref, *refs):
    total_ref, out_ref, held, arrived = refs[-4:]
    count = (len(refs) - 4) // 2
    copies = []
    for k in range(count):
        start = refs[k].shape[0] - held.shape[1]
        copies.append(
            pltpu.make_async_copy(refs[k].at[pl.ds(start, held.shape[1])], held.at[k], arrived.at[k])
        )
        copies[-1].start()
    total = total_ref[...]
    for k in range(count):
        copies[k].wait()
        total += lax.dot_general(
            held[k], refs[count + k][0], (((1,), (1,)), ((), ())), preferred_element_type=F32
        )
    out_ref[...] = total


def add_grads(pieces, origins, wide_grads, total, n_dp):
    directions, units = total.shape[0], pieces[0].shape[1]
    n_mp, tokens, _ = wide_grads.shape
    share = n_dp // n_mp
    count = len(pieces)
    at = jnp.stack([f(origin, share) for origin in origins for f in (jnp.floor_divide, jnp.remainder)])

    def columns(k):
        return pl.BlockSpec((1, tokens, units), lambda i, at_ref: (at_ref[2 * k], 0, at_ref[2 * k + 1]))

    return pl.pallas_call(
        add_grads_kernel,
        grid_spec=pltpu.PrefetchScalarGridSpec(
            num_scalar_prefetch=1,
            grid=(1,),
            in_specs=[pl.BlockSpec(memory_space=pl.ANY)] * count
            + [columns(k) for k in range(count)]
            + [whole_block(total.shape)],
            out_specs=whole_block(total.shape),
            scratch_shapes=[
                pltpu.VMEM((count, directions, units), BF16),
                pltpu.SemaphoreType.DMA((count,)),
            ],
        ),
        out_shape=jax.ShapeDtypeStruct(total.shape, F32),
        compiler_params=pltpu.CompilerParams(vmem_limit_bytes=VMEM_BYTES),
        cost_estimate=pl.CostEstimate(flops=1, bytes_accessed=1, transcendentals=0),
        name="add_grads",
    )(at.astype(jnp.int32), *pieces, *[wide_grads] * count, total)


def join_kernel(at_ref, early_ref, late_ref, out_ref):
    count = early_ref.shape[0]
    for k in range(count):
        out_ref[at_ref[k]] = early_ref[k]
    out_ref[at_ref[count]] = late_ref[0]


def join(early, late, at):
    whole = pl.BlockSpec(memory_space=pltpu.VMEM)
    return pl.pallas_call(
        join_kernel,
        in_specs=[pl.BlockSpec(memory_space=pltpu.SMEM), whole, whole],
        out_specs=whole,
        out_shape=jax.ShapeDtypeStruct((early.shape[0] + 1,) + early.shape[1:], early.dtype),
        name="join_pairs",
    )(at, early, late)


def expand_kernel(tiles, rows, at_ref, near_ref, far_ref, turn_ref, *refs):
    count = (len(refs) - 9) // 2
    owns, others, out_ref = refs[:count], refs[count : 2 * count], refs[2 * count]
    scaled, turned, back, held, pieces, sent, first_sem, piece_sem, out_sem = refs[-9:]
    deep = pieces.shape[2]
    ahead = min(AHEAD, tiles)
    depth, lanes = near_ref.shape[0], pieces.shape[3]
    out_rows = sent.shape[1]

    def fetch(group, half, t):
        tile = half * tiles + t
        return [
            pltpu.make_async_copy(ref.at[pl.ds(t * deep, deep)], pieces.at[tile, k], piece_sem.at[tile, k])
            for k, ref in enumerate(group)
        ]

    def store(half, t):
        side = at_ref[0] if half == 0 else 1 - at_ref[0]
        tile = half * tiles + t
        return pltpu.make_async_copy(
            sent.at[tile % 2], out_ref.at[pl.ds((side * tiles + t) * out_rows, out_rows)], out_sem.at[tile % 2]
        )

    opening = [
        pltpu.make_async_copy(near_ref, scaled.at[0], first_sem.at[0]),
        pltpu.make_async_copy(far_ref, scaled.at[1], first_sem.at[1]),
        pltpu.make_async_copy(turn_ref, turned, first_sem.at[2]),
    ]
    for copy in opening:
        copy.start()
    for t in range(ahead):
        for copy in fetch(owns, 0, t):
            copy.start()
    for copy in opening:
        copy.wait()
    dims = (((0,), (0,)), ((), ()))
    total = lax.dot_general(scaled[0], turned[:depth], dims, preferred_element_type=F32)
    total += lax.dot_general(scaled[1], turned[depth:], dims, preferred_element_type=F32)
    back[...] = total.astype(BF16)
    for k in range(count):
        start = pl.multiple_of(at_ref[1 + k] * rows, 16)
        held[k * rows : (k + 1) * rows] = back[pl.ds(start, rows)]

    def step(half, group, t, more, next_half, next_group, next_t, settled):
        if more:
            for copy in fetch(next_group, next_half, next_t):
                copy.start()
        for copy in fetch(group, half, t):
            copy.wait()
        tile = half * tiles + t
        if settled is not None:
            store(*settled).wait()
        for c in range(deep // rows):
            part = jnp.concatenate([pieces[tile, k, c * rows : (c + 1) * rows] for k in range(count)], axis=0)
            sent[tile % 2, c * lanes : (c + 1) * lanes] = lax.dot_general(
                part, held[...], dims, preferred_element_type=F32
            ).astype(BF16)
        store(half, t).start()

    for half, group in ((0, owns), (1, others)):
        for t in range(tiles):
            tile = half * tiles + t
            coming = tile + ahead
            before = tile - 2
            step(
                half,
                group,
                t,
                coming < 2 * tiles,
                coming // tiles,
                owns if coming < tiles else others,
                coming % tiles,
                (before // tiles, before % tiles) if before >= 0 else None,
            )
    for tile in (2 * tiles - 2, 2 * tiles - 1):
        store(tile // tiles, tile % tiles).wait()


def expand(owns, others, pairs, rows, units, core, near, far, turn):
    lanes = owns[0].shape[1]
    chunks = units // 2 // lanes
    columns = turn.shape[1]
    at = jnp.stack([core] + list(pairs)).astype(jnp.int32)
    if rows % 16:
        wide = jnp.concatenate([near, far])
        back = lax.dot_general(wide, turn, (((0,), (0,)), ((), ())), preferred_element_type=F32).astype(BF16)
        held = jnp.take(back.reshape((-1, rows, columns)), at[1:], axis=0).reshape((-1, columns))
        sides = []
        for pieces in (owns, others):
            plain = jnp.concatenate([unchunk(piece, rows, chunks) for piece in pieces])
            sides.append(lax.dot_general(plain, held, (((0,), (0,)), ((), ())), preferred_element_type=F32).astype(BF16))
        return jnp.where(core == 0, jnp.concatenate(sides), jnp.concatenate(sides[::-1]))
    group = max(g for g in range(1, chunks + 1) if chunks % g == 0 and g * lanes <= EXPAND_ROWS)
    tiles = chunks // group
    count = len(owns)
    anywhere = pl.BlockSpec(memory_space=pl.ANY)
    return pl.pallas_call(
        functools.partial(expand_kernel, tiles, rows),
        grid_spec=pltpu.PrefetchScalarGridSpec(
            num_scalar_prefetch=1,
            grid=(1,),
            in_specs=[anywhere] * (3 + 2 * count),
            out_specs=anywhere,
            scratch_shapes=[
                pltpu.VMEM((2,) + near.shape, BF16),
                pltpu.VMEM(turn.shape, BF16),
                pltpu.VMEM((count * rows, columns), BF16),
                pltpu.VMEM((count * rows, columns), BF16),
                pltpu.VMEM((2 * tiles, count, group * rows, lanes), BF16),
                pltpu.VMEM((2, group * lanes, columns), BF16),
                pltpu.SemaphoreType.DMA((3,)),
                pltpu.SemaphoreType.DMA((2 * tiles, count)),
                pltpu.SemaphoreType.DMA((2,)),
            ],
        ),
        out_shape=jax.ShapeDtypeStruct((units, columns), BF16),
        compiler_params=pltpu.CompilerParams(vmem_limit_bytes=VMEM_BYTES),
        cost_estimate=pl.CostEstimate(
            flops=2 * rows * count * units * columns, bytes_accessed=2 * units * columns, transcendentals=0
        ),
        name="expand_update",
    )(at, near, far, turn, *owns, *others)


def gather_near_first(x, axis_name):
    x = x[None]
    for bit in bits(axis_name):
        x = jnp.concatenate([x, flip(x, axis_name, bit)], axis=0)
    return x


def near_first(x, axis, me):
    size = x.shape[axis]
    for k in range(size.bit_length() - 1):
        shape = x.shape[:axis] + (size >> (k + 1), 2, 1 << k) + x.shape[axis + 1 :]
        parts = x.reshape(shape)
        swapped = jnp.flip(parts, axis + 1)
        x = jnp.where((me >> k) % 2 == 1, swapped, parts).reshape(x.shape)
    return x


def products(g, a):
    dims = (((1,), (1,)), ((), ()))
    g = g.astype(BF16)
    g_sq = (g.astype(F32) ** 2).astype(BF16)
    a_sq = (a.astype(F32) ** 2).astype(BF16)
    return (
        lax.dot_general(g, a, dims, preferred_element_type=F32),
        lax.dot_general(g_sq, a_sq, dims, preferred_element_type=F32),
    )


def picked(me_ref, g_ref, flipped):
    pairs = g_ref.shape[0] // 2
    core, pair = me_ref[0] % 2, me_ref[0] // 2
    return jnp.concatenate(
        [g_ref[(pair ^ r) * 2 + (core ^ flipped)] for r in range(pairs)], axis=0
    )


def theirs_kernel(rows, me_ref, at_ref, g_ref, *refs):
    out_ref, a_ref = refs[-2:]
    count = len(refs) // 2 - 1
    k = 0
    for own_ref, got_ref in zip(refs[:count], refs[count:-2]):
        total = (own_ref[...] + got_ref[...].astype(F32)).astype(BF16)
        for i in range(total.shape[0] // rows):
            start = pl.multiple_of(at_ref[k] * rows, 16)
            a_ref[pl.ds(start, rows)] = total[i * rows : (i + 1) * rows]
            k += 1
    rotated, squares = products(picked(me_ref, g_ref, 1), a_ref[...])
    out_ref[0] = rotated.astype(BF16)
    out_ref[1] = squares.astype(BF16)


def ours_kernel(me_ref, g_ref, a_ref, got_ref, *out_refs):
    width = g_ref.shape[1]
    rotated, squares = products(picked(me_ref, g_ref, 0), a_ref[...])
    rotated += got_ref[0].astype(F32)
    squares += got_ref[1].astype(F32)
    for r, out_ref in enumerate(out_refs):
        out_ref[0] = rotated[r * width : (r + 1) * width].astype(BF16)
        out_ref[1] = squares[r * width : (r + 1) * width].astype(BF16)


def token_sums(grad_proj_t, sums, gots, order, pair_rows):
    blocks, width, tokens = grad_proj_t.shape
    pairs = blocks // 2
    top = lax.axis_size("dp") // blocks
    assert top == 2
    rows = len(order) * pair_rows
    order = jnp.stack(order).astype(jnp.int32)
    me = lax.axis_index("dp") % blocks
    whole = pl.BlockSpec(memory_space=pltpu.VMEM)
    if width % 16 == 0 and pair_rows % 16 == 0 and gots:
        params = pltpu.CompilerParams(vmem_limit_bytes=VMEM_BYTES)
        cost = pl.CostEstimate(
            flops=2 * blocks * width * rows * tokens,
            bytes_accessed=4 * blocks * width * tokens + 2 * rows * tokens + 2 * blocks * width * rows,
            transcendentals=0,
        )
        index = me.astype(jnp.int32).reshape((1,))
        index_spec = pl.BlockSpec(memory_space=pltpu.SMEM)
        sent, act_proj_t = pl.pallas_call(
            functools.partial(theirs_kernel, pair_rows),
            in_specs=[index_spec, index_spec, whole] + [whole] * (len(sums) + len(gots)),
            out_specs=[whole, whole],
            out_shape=[
                jax.ShapeDtypeStruct((2, pairs * width, rows), BF16),
                jax.ShapeDtypeStruct((rows, tokens), BF16),
            ],
            compiler_params=params,
            cost_estimate=cost,
            name="sums_for_other_core",
        )(index, order, grad_proj_t, *sums, *gots)
        got = flip(sent, "dp", 1)
        ours = pl.pallas_call(
            ours_kernel,
            in_specs=[index_spec, whole, whole, whole],
            out_specs=[whole] * pairs,
            out_shape=[jax.ShapeDtypeStruct((2, width, rows), BF16)] * pairs,
            compiler_params=params,
            cost_estimate=cost,
            name="sums_for_own_core",
        )(index, grad_proj_t, act_proj_t, got)
    else:
        act_proj_t = jnp.concatenate(sums)
        for bit in bits("mp"):
            act_proj_t = act_proj_t + flip(act_proj_t.astype(BF16), "mp", bit).astype(F32)
        act_proj_t = act_proj_t.astype(BF16).reshape((-1, pair_rows, tokens))
        act_proj_t = join(act_proj_t[:-1], act_proj_t[-1:], order).reshape((-1, tokens))
        near = near_first(near_first(grad_proj_t.reshape((pairs, 2, width, tokens)), 0, me // 2), 1, me % 2)
        near = near.transpose(1, 0, 2, 3).reshape((2 * pairs * width, tokens))
        both = jnp.stack(products(near, act_proj_t)).reshape((2, 2, pairs, width, rows))
        total = both[:, 0] + flip(both[:, 1].astype(BF16), "dp", 1).astype(F32)
        ours = [total[:, r].astype(BF16) for r in range(pairs)]
    total = ours[0].astype(F32)
    for r in range(1, pairs):
        total += flip(ours[r], "dp", 2 * r).astype(F32)
    total += flip(total.astype(BF16), "dp", blocks).astype(F32)
    return total[0], total[1]


def gather_scaled(scaled, diag):
    pairs = lax.axis_size("dp") // 4
    x = gather_near_first(scaled, "mp")
    x = jnp.stack([x] + [flip(x, "dp", 2 * r) for r in range(1, pairs)])
    x, diag = lax.optimization_barrier((x, diag))
    return x, flip(x, "dp", 1), diag


def place_diag(diag_t):
    n_dp, n_mp = lax.axis_size("dp"), lax.axis_size("mp")
    width, rows = diag_t.shape[0], diag_t.shape[1] // n_mp
    share, blocks = n_mp // 2, n_dp // 2
    here, me = lax.axis_index("mp"), lax.axis_index("dp")
    block = here * blocks + me % blocks
    out = jnp.zeros((share, width, rows), diag_t.dtype)
    for k in range(share):
        hops = []
        for m in range(n_mp):
            for i in range(n_dp):
                b = m * blocks + i % blocks
                hops.append((i * n_mp + m, (b // share) * n_mp + 2 * ((b + k) % share) + i // blocks))
        target = 2 * ((block + k) % share) + me // blocks
        sent = lax.dynamic_slice(diag_t, (0, target * rows), (width, rows))
        got = lax.ppermute(sent, ("dp", "mp"), hops)
        out = lax.dynamic_update_slice(out, got[None], ((here // 2 - k) % share, 0, 0))
    return out.reshape((share * width, rows)).T


def on_device(acts, grads, basis_in, basis_out, damping):
    tok_rows = acts.shape[0]
    n_dp, n_mp = lax.axis_size("dp"), lax.axis_size("mp")
    me = lax.axis_index("dp")
    tokens_all = tok_rows * n_dp
    out_units, directions = basis_out.shape
    width = directions // n_dp

    core, half = me % 2, n_dp // 2
    units = acts.shape[1]
    chunks = units // 2 // out_units
    own_rows = basis_in.shape[1]
    mine = basis_in.T

    def side_of(side):
        part = lax.dynamic_slice(mine, (0, side * (units // 2)), (own_rows, units // 2))
        return jnp.stack([part[:, c * out_units : (c + 1) * out_units] for c in range(chunks)])

    kept = side_of(core)
    got = flip(side_of(1 - core), "dp", 1)
    both = jnp.stack([jnp.where(core == 0, kept, got), jnp.where(core == 0, got, kept)], axis=1)
    rows = 2 * own_rows
    in_rows = chunks * rows
    basis_out_t = basis_out.T
    own_piece = jnp.concatenate([both.reshape((in_rows, out_units)), basis_out_t])

    wide_grads = gather_doubling(grads, "mp")

    ahead, back_hops = ring_hops(n_dp)
    everyone = (ahead[0] + back_hops[1], back_hops[0] + ahead[1])
    began = ring_place("dp")
    grad_proj_t = jnp.zeros((directions, tok_rows), F32)
    owns, others, pairs, sums, gots = [], [], [], [], []
    rows_near = basis_out_t

    def take_grads(pieces, where_from):
        nonlocal grad_proj_t
        origins = [2 * p + core for p in where_from] + [2 * p + 1 - core for p in where_from]
        grad_proj_t = add_grads(pieces, origins, wide_grads, grad_proj_t, n_dp)

    def use(pieces, where_from, grads_too=True, costed=False, known=()):
        fresh = [flip(piece, "dp", 1) for piece in pieces[len(known) :]]
        swapped = list(known) + fresh[::-1]
        sums.append(project(pieces, swapped, rows, core, acts, costed))
        gots.append([flip(sums[-1].astype(BF16), "mp", 1)] if n_mp == 2 else [])
        owns.extend(pieces)
        others.extend(swapped)
        pairs.extend(where_from)
        if grads_too:
            take_grads(pieces + swapped, where_from)

    moving = [own_piece, own_piece]
    waiting = [own_piece], [me // 2]
    for step in range(1, half // 2):
        moving = [lax.ppermute(x, "dp", everyone[k]) for k, x in enumerate(moving)]
        if step == 1:
            swapped = flip(own_piece, "dp", 1)
            moving, own_piece, swapped = lax.optimization_barrier((moving, own_piece, swapped))
            waiting = [own_piece], [me // 2]
        else:
            use(*waiting, known=[swapped] if step == 2 else [])
            moving, sums[-1], gots[:-1], grad_proj_t, rows_near = lax.optimization_barrier(
                (moving, sums[-1], gots[:-1], grad_proj_t, rows_near)
            )
            waiting = [], []
        if step == min(2, half // 2 - 1):
            rows_near = gather_near_first(rows_near, "mp")
        way = (1 - 2 * core) * step
        waiting = waiting[0] + moving, waiting[1] + [began(way), began(-way)]

    last = lax.ppermute(moving[0][:in_rows], "dp", everyone[0])
    held = moving[0][in_rows:]
    use(*waiting)
    held, last, sums[-1], gots[:-1], grad_proj_t = lax.optimization_barrier(
        (held, last, sums[-1], gots[:-1], grad_proj_t)
    )
    last_out = lax.ppermute(held, "dp", everyone[0])
    last_pair = began(half // 2)
    use([last], [last_pair], False, True)
    last_out, sums[-1], gots[:-1] = lax.optimization_barrier((last_out, sums[-1], gots[:-1]))
    grad_proj_t = add_grads(
        [last_out, flip(last_out, "dp", 1)],
        [2 * last_pair + core, 2 * last_pair + 1 - core],
        wide_grads,
        grad_proj_t,
        n_dp,
    )

    rows_near = rows_near.reshape((n_mp, half // 2, 2, 2 * width, out_units))
    rows_near = near_first(near_first(rows_near, 1, (me // 2) % (half // 2)), 2, core)
    rows_near = rows_near.transpose(2, 1, 0, 3, 4).reshape((n_mp * directions, out_units))

    rotated, squares = token_sums(
        grad_proj_t.reshape((half, 2 * width, tok_rows)), sums, [got for part in gots for got in part], pairs, rows
    )
    diag_t = squares / tokens_all
    scaled = (rotated / (diag_t + damping[0])).astype(BF16)
    near, far, diag = gather_scaled(scaled, place_diag(diag_t))
    near, far = (x.reshape((directions * n_mp // 2, -1)) for x in (near, far))
    return (expand(owns, others, pairs, rows, units, core, near, far, rows_near), diag)


def solution(mesh):
    placed = (P("dp", "mp"), P("dp", "mp"), P("mp", "dp"), P("dp", "mp"), P())
    return jax.shard_map(
        on_device,
        mesh=mesh,
        in_specs=placed,
        out_specs=(P("mp", "dp"), P("mp", "dp")),
        check_vma=False,
    )
```

```python
import functools

import jax
import jax.numpy as jnp
from jax import lax
from jax.experimental import pallas as pl
from jax.experimental.pallas import tpu as pltpu
from jax.sharding import PartitionSpec as P

BF16, F32 = jnp.bfloat16, jnp.float32
VMEM_BYTES = 48 * 1024 * 1024
FIRST = 2
AHEAD = 3
PROJECT_UNITS = 8192


def flip(x, axis_name, bit):
    size = lax.axis_size(axis_name)
    return lax.ppermute(x, axis_name, [(i, i ^ bit) for i in range(size)])


def bits(axis_name):
    size = lax.axis_size(axis_name)
    assert size & (size - 1) == 0
    return [1 << k for k in range(size.bit_length() - 1)]


def gather_doubling(x, axis_name):
    me = lax.axis_index(axis_name)
    x = x[None]
    for bit in reversed(bits(axis_name)):
        other = flip(x, axis_name, bit)
        side = (me // bit) % 2
        low = jnp.where(side == 0, x, other)
        high = jnp.where(side == 0, other, x)
        x = jnp.stack([low, high], axis=1).reshape((2 * x.shape[0],) + x.shape[1:])
    return x


def ring_hops(size):
    half = size // 2
    order = list(range(0, half, 2)) + list(range(half - 1, 0, -2))
    hops = [(order[k], order[(k + 1) % half]) for k in range(half)]
    ahead = [[(2 * s + c, 2 * d + c) for s, d in hops] for c in (0, 1)]
    return ahead, [[(d, s) for s, d in part] for part in ahead]


def ring_place(axis_name):
    half = lax.axis_size(axis_name) // 2
    pair = lax.axis_index(axis_name) // 2
    place = jnp.where(pair % 2 == 0, pair // 2, half - (pair + 1) // 2)

    def began(step):
        p = (place - step) % half
        return jnp.where(p < half // 2, 2 * p, 2 * (half - p) - 1)

    return began


def tile_of(extent, most):
    return max(t for t in range(128, most + 1, 128) if extent % t == 0)


def whole_block(shape):
    return pl.BlockSpec(shape, lambda *_: (0,) * len(shape))


def halves_spec(shape, tiles, second):
    if second:
        return pl.BlockSpec(shape, lambda i, *_: (jnp.maximum(i - tiles, 0), 0))
    return pl.BlockSpec(shape, lambda i, *_: (jnp.minimum(i, tiles - 1), 0))


def tile_index(i, tiles, at_ref):
    return jnp.where(i < tiles, at_ref[0], 1 - at_ref[0]) * tiles + i % tiles


def project_kernel(tiles, rows, at_ref, acts_ref, *refs):
    sums_ref, held = refs[-2:]
    count = len(refs) // 2 - 1
    step = pl.program_id(0)
    lanes = refs[0].shape[1]

    @pl.when(step == 0)
    def _():
        held[...] = jnp.zeros_like(held)

    def add(pieces):
        total = held[...]
        for c in range(pieces[0].shape[0] // rows):
            part = jnp.concatenate([piece[c * rows : (c + 1) * rows] for piece in pieces], axis=0)
            total += lax.dot_general(
                acts_ref[:, c * lanes : (c + 1) * lanes],
                part,
                (((1,), (1,)), ((), ())),
                preferred_element_type=F32,
            )
        held[...] = total

    pl.when(step < tiles)(lambda: add(refs[:count]))
    pl.when(step >= tiles)(lambda: add(refs[count:-2]))

    @pl.when(step == 2 * tiles - 1)
    def _():
        sums_ref[...] = held[...].T


def project(owns, others, rows, core, acts, costed=False):
    tokens, units = acts.shape
    lanes = owns[0].shape[1]
    chunks = units // 2 // lanes
    if rows % 16:
        total = 0
        for pieces, side in ((owns, core), (others, 1 - core)):
            half = lax.dynamic_slice(acts, (0, side * (units // 2)), (tokens, units // 2))
            plain = [unchunk(piece, rows, chunks) for piece in pieces]
            total += jnp.concatenate(
                [lax.dot_general(p, half, (((1,), (1,)), ((), ())), preferred_element_type=F32) for p in plain]
            )
        return total
    group = max(g for g in range(1, chunks + 1) if chunks % g == 0 and g * lanes <= PROJECT_UNITS)
    tiles = chunks // group
    return pl.pallas_call(
        functools.partial(project_kernel, tiles, rows),
        grid_spec=pltpu.PrefetchScalarGridSpec(
            num_scalar_prefetch=1,
            grid=(2 * tiles,),
            in_specs=[pl.BlockSpec((tokens, group * lanes), lambda i, at_ref: (0, tile_index(i, tiles, at_ref)))]
            + [halves_spec((group * rows, lanes), tiles, False)] * len(owns)
            + [halves_spec((group * rows, lanes), tiles, True)] * len(owns),
            out_specs=whole_block((len(owns) * rows, tokens)),
            scratch_shapes=[pltpu.VMEM((tokens, len(owns) * rows), F32)],
        ),
        out_shape=jax.ShapeDtypeStruct((len(owns) * rows, tokens), F32),
        compiler_params=pltpu.CompilerParams(vmem_limit_bytes=VMEM_BYTES),
        cost_estimate=pl.CostEstimate(
            flops=2 * len(owns) * rows * units * tokens if costed else 1,
            bytes_accessed=2 * units * (len(owns) * rows + tokens) if costed else 1,
            transcendentals=0,
        ),
        name="project_acts",
    )(core.astype(jnp.int32).reshape((1,)), acts, *owns, *others)


def unchunk(piece, rows, chunks):
    lanes = piece.shape[1]
    return piece[: chunks * rows].reshape((chunks, rows, lanes)).transpose(1, 0, 2).reshape((rows, -1))


def add_grads_kernel(apart, at_ref, *refs):
    total_ref, out_ref, held, arrived = refs[-4:]
    count = (len(refs) - 4) // 2
    copies = []
    if apart:
        early = pltpu.make_async_copy(total_ref, out_ref, arrived.at[count])
        early.start()
    for k in range(count):
        start = refs[k].shape[0] - held.shape[1]
        copies.append(
            pltpu.make_async_copy(refs[k].at[pl.ds(start, held.shape[1])], held.at[k], arrived.at[k])
        )
        copies[-1].start()
    total = jnp.zeros(out_ref.shape, F32) if apart else total_ref[...]
    for k in range(count):
        copies[k].wait()
        total += lax.dot_general(
            held[k], refs[count + k][0], (((1,), (1,)), ((), ())), preferred_element_type=F32
        )
    if apart:
        early.wait()
        total += out_ref[...]
    out_ref[...] = total


def add_grads(pieces, origins, wide_grads, total, n_dp, apart=False):
    directions, units = total.shape[0], pieces[0].shape[1]
    n_mp, tokens, _ = wide_grads.shape
    share = n_dp // n_mp
    count = len(pieces)
    at = jnp.stack([f(origin, share) for origin in origins for f in (jnp.floor_divide, jnp.remainder)])

    def columns(k):
        return pl.BlockSpec((1, tokens, units), lambda i, at_ref: (at_ref[2 * k], 0, at_ref[2 * k + 1]))

    return pl.pallas_call(
        functools.partial(add_grads_kernel, apart),
        grid_spec=pltpu.PrefetchScalarGridSpec(
            num_scalar_prefetch=1,
            grid=(1,),
            in_specs=[pl.BlockSpec(memory_space=pl.ANY)] * count
            + [columns(k) for k in range(count)]
            + [pl.BlockSpec(memory_space=pltpu.HBM) if apart else whole_block(total.shape)],
            out_specs=whole_block(total.shape),
            scratch_shapes=[
                pltpu.VMEM((count, directions, units), BF16),
                pltpu.SemaphoreType.DMA((count + 1,)),
            ],
        ),
        out_shape=jax.ShapeDtypeStruct(total.shape, F32),
        compiler_params=pltpu.CompilerParams(vmem_limit_bytes=VMEM_BYTES),
        cost_estimate=pl.CostEstimate(flops=1, bytes_accessed=1, transcendentals=0),
        name="add_grads",
    )(at.astype(jnp.int32), *pieces, *[wide_grads] * count, total)


def join_kernel(at_ref, early_ref, late_ref, out_ref):
    count = early_ref.shape[0]
    for k in range(count):
        out_ref[at_ref[k]] = early_ref[k]
    out_ref[at_ref[count]] = late_ref[0]


def join(early, late, at):
    whole = pl.BlockSpec(memory_space=pltpu.VMEM)
    return pl.pallas_call(
        join_kernel,
        in_specs=[pl.BlockSpec(memory_space=pltpu.SMEM), whole, whole],
        out_specs=whole,
        out_shape=jax.ShapeDtypeStruct((early.shape[0] + 1,) + early.shape[1:], early.dtype),
        name="join_pairs",
    )(at, early, late)


def expand_kernel(tiles, rows, at_ref, near_ref, far_ref, turn_ref, _, *refs):
    count = (len(refs) - 11) // 2
    groups, out_ref = (refs[:count], refs[count : 2 * count]), refs[2 * count]
    scaled, turned, back, held, pieces, sent, first_sem, piece_sem, out_sem = refs[-9:]
    depth, lanes = near_ref.shape[0], pieces.shape[3]
    half_units = out_ref.shape[0] // 2

    def fetch(n):
        half, first, chunks = tiles[n]
        part = pl.ds(first * rows, chunks * rows)
        return [
            pltpu.make_async_copy(ref.at[part], pieces.at[half, k, part], piece_sem.at[n, k])
            for k, ref in enumerate(groups[half])
        ]

    def store(n):
        half, first, chunks = tiles[n]
        side = at_ref[0] if half == 0 else 1 - at_ref[0]
        return pltpu.make_async_copy(
            sent.at[n % 2, pl.ds(0, chunks * lanes)],
            out_ref.at[pl.ds(side * half_units + first * lanes, chunks * lanes)],
            out_sem.at[n % 2],
        )

    opening = [
        pltpu.make_async_copy(near_ref, scaled.at[0], first_sem.at[0]),
        pltpu.make_async_copy(far_ref, scaled.at[1], first_sem.at[1]),
        pltpu.make_async_copy(turn_ref, turned, first_sem.at[2]),
    ]
    for copy in opening + fetch(0):
        copy.start()
    for copy in opening:
        copy.wait()
    for n in range(1, AHEAD):
        for copy in fetch(n):
            copy.start()
    dims = (((0,), (0,)), ((), ()))
    total = lax.dot_general(scaled[0], turned[:depth], dims, preferred_element_type=F32)
    total += lax.dot_general(scaled[1], turned[depth:], dims, preferred_element_type=F32)
    back[...] = total.astype(BF16)
    for k in range(count):
        start = pl.multiple_of(at_ref[1 + k] * rows, 16)
        held[k * rows : (k + 1) * rows] = back[pl.ds(start, rows)]

    for n, (half, first, chunks) in enumerate(tiles):
        if n + AHEAD < len(tiles):
            for copy in fetch(n + AHEAD):
                copy.start()
        for copy in fetch(n):
            copy.wait()
        if n >= 2:
            store(n - 2).wait()
        for c in range(chunks):
            at = (first + c) * rows
            part = jnp.concatenate([pieces[half, k, at : at + rows] for k in range(count)], axis=0)
            sent[n % 2, c * lanes : (c + 1) * lanes] = lax.dot_general(
                part, held[...], dims, preferred_element_type=F32
            ).astype(BF16)
        store(n).start()
    store(len(tiles) - 2).wait()
    store(len(tiles) - 1).wait()


def expand(owns, others, pairs, rows, units, core, near, far, turn, diag_t):
    lanes = owns[0].shape[1]
    chunks = units // 2 // lanes
    columns = turn.shape[1]
    at = jnp.stack([core] + list(pairs)).astype(jnp.int32)
    if rows % 16:
        wide = jnp.concatenate([near, far])
        back = lax.dot_general(wide, turn, (((0,), (0,)), ((), ())), preferred_element_type=F32).astype(BF16)
        held = jnp.take(back.reshape((-1, rows, columns)), at[1:], axis=0).reshape((-1, columns))
        sides = []
        for pieces in (owns, others):
            plain = jnp.concatenate([unchunk(piece, rows, chunks) for piece in pieces])
            sides.append(lax.dot_general(plain, held, (((0,), (0,)), ((), ())), preferred_element_type=F32).astype(BF16))
        return jnp.where(core == 0, jnp.concatenate(sides), jnp.concatenate(sides[::-1])), diag_t
    size = max(1, (chunks - FIRST) // 2)
    cuts = sorted({0, min(FIRST, chunks)} | set(range(FIRST, chunks, size)) | {chunks})
    spans = [(low, high - low) for low, high in zip(cuts, cuts[1:])]
    tiles = [(0, low, n) for low, n in spans] + [(1, chunks - low - n, n) for low, n in spans[::-1]]
    count = len(owns)
    anywhere = pl.BlockSpec(memory_space=pl.ANY)
    return pl.pallas_call(
        functools.partial(expand_kernel, tiles, rows),
        grid_spec=pltpu.PrefetchScalarGridSpec(
            num_scalar_prefetch=1,
            grid=(1,),
            in_specs=[anywhere] * 3 + [pl.BlockSpec(memory_space=pltpu.HBM)] + [anywhere] * (2 * count),
            out_specs=[anywhere, pl.BlockSpec(memory_space=pltpu.HBM)],
            scratch_shapes=[
                pltpu.VMEM((2,) + near.shape, BF16),
                pltpu.VMEM(turn.shape, BF16),
                pltpu.VMEM((count * rows, columns), BF16),
                pltpu.VMEM((count * rows, columns), BF16),
                pltpu.VMEM((2, count, chunks * rows, lanes), BF16),
                pltpu.VMEM((2, max(n for _, _, n in tiles) * lanes, columns), BF16),
                pltpu.SemaphoreType.DMA((3,)),
                pltpu.SemaphoreType.DMA((len(tiles), count)),
                pltpu.SemaphoreType.DMA((2,)),
            ],
        ),
        out_shape=[jax.ShapeDtypeStruct((units, columns), BF16), jax.ShapeDtypeStruct(diag_t.shape, F32)],
        input_output_aliases={4: 1},
        compiler_params=pltpu.CompilerParams(vmem_limit_bytes=VMEM_BYTES),
        cost_estimate=pl.CostEstimate(
            flops=2 * rows * count * units * columns, bytes_accessed=2 * units * columns, transcendentals=0
        ),
        name="expand_update",
    )(at, near, far, turn, diag_t, *owns, *others)


def gather_near_first(x, axis_name):
    x = x[None]
    for bit in bits(axis_name):
        x = jnp.concatenate([x, flip(x, axis_name, bit)], axis=0)
    return x


def near_first(x, axis, me):
    size = x.shape[axis]
    for k in range(size.bit_length() - 1):
        shape = x.shape[:axis] + (size >> (k + 1), 2, 1 << k) + x.shape[axis + 1 :]
        parts = x.reshape(shape)
        swapped = jnp.flip(parts, axis + 1)
        x = jnp.where((me >> k) % 2 == 1, swapped, parts).reshape(x.shape)
    return x


def products(g, a):
    dims = (((1,), (1,)), ((), ()))
    g = g.astype(BF16)
    g_sq = (g.astype(F32) ** 2).astype(BF16)
    a_sq = (a.astype(F32) ** 2).astype(BF16)
    return (
        lax.dot_general(g, a, dims, preferred_element_type=F32),
        lax.dot_general(g_sq, a_sq, dims, preferred_element_type=F32),
    )


def picked(me_ref, g_ref, flipped):
    pairs = g_ref.shape[0] // 2
    core, pair = me_ref[0] % 2, me_ref[0] // 2
    return jnp.concatenate(
        [g_ref[(pair ^ r) * 2 + (core ^ flipped)] for r in range(pairs)], axis=0
    )


def theirs_kernel(rows, me_ref, at_ref, g_ref, *refs):
    out_ref, a_ref = refs[-2:]
    count = len(refs) // 2 - 1
    k = 0
    for own_ref, got_ref in zip(refs[:count], refs[count:-2]):
        total = (own_ref[...] + got_ref[...].astype(F32)).astype(BF16)
        for i in range(total.shape[0] // rows):
            start = pl.multiple_of(at_ref[k] * rows, 16)
            a_ref[pl.ds(start, rows)] = total[i * rows : (i + 1) * rows]
            k += 1
    rotated, squares = products(picked(me_ref, g_ref, 1), a_ref[...])
    out_ref[0] = rotated.astype(BF16)
    out_ref[1] = squares.astype(BF16)


def ours_kernel(me_ref, g_ref, a_ref, got_ref, *out_refs):
    width = g_ref.shape[1]
    rotated, squares = products(picked(me_ref, g_ref, 0), a_ref[...])
    rotated += got_ref[0].astype(F32)
    squares += got_ref[1].astype(F32)
    for r, out_ref in enumerate(out_refs):
        out_ref[0] = rotated[r * width : (r + 1) * width].astype(BF16)
        out_ref[1] = squares[r * width : (r + 1) * width].astype(BF16)


def token_sums(grad_proj_t, sums, gots, order, pair_rows):
    blocks, width, tokens = grad_proj_t.shape
    pairs = blocks // 2
    top = lax.axis_size("dp") // blocks
    assert top == 2
    rows = len(order) * pair_rows
    order = jnp.stack(order).astype(jnp.int32)
    me = lax.axis_index("dp") % blocks
    whole = pl.BlockSpec(memory_space=pltpu.VMEM)
    if width % 16 == 0 and pair_rows % 16 == 0 and gots:
        params = pltpu.CompilerParams(vmem_limit_bytes=VMEM_BYTES)
        cost = pl.CostEstimate(
            flops=2 * blocks * width * rows * tokens,
            bytes_accessed=4 * blocks * width * tokens + 2 * rows * tokens + 2 * blocks * width * rows,
            transcendentals=0,
        )
        index = me.astype(jnp.int32).reshape((1,))
        index_spec = pl.BlockSpec(memory_space=pltpu.SMEM)
        sent, act_proj_t = pl.pallas_call(
            functools.partial(theirs_kernel, pair_rows),
            in_specs=[index_spec, index_spec, whole] + [whole] * (len(sums) + len(gots)),
            out_specs=[whole, whole],
            out_shape=[
                jax.ShapeDtypeStruct((2, pairs * width, rows), BF16),
                jax.ShapeDtypeStruct((rows, tokens), BF16),
            ],
            compiler_params=params,
            cost_estimate=cost,
            name="sums_for_other_core",
        )(index, order, grad_proj_t, *sums, *gots)
        got = flip(sent, "dp", 1)
        ours = pl.pallas_call(
            ours_kernel,
            in_specs=[index_spec, whole, whole, whole],
            out_specs=[whole] * pairs,
            out_shape=[jax.ShapeDtypeStruct((2, width, rows), BF16)] * pairs,
            compiler_params=params,
            cost_estimate=cost,
            name="sums_for_own_core",
        )(index, grad_proj_t, act_proj_t, got)
    else:
        act_proj_t = jnp.concatenate(sums)
        for bit in bits("mp"):
            act_proj_t = act_proj_t + flip(act_proj_t.astype(BF16), "mp", bit).astype(F32)
        act_proj_t = act_proj_t.astype(BF16).reshape((-1, pair_rows, tokens))
        act_proj_t = join(act_proj_t[:-1], act_proj_t[-1:], order).reshape((-1, tokens))
        near = near_first(near_first(grad_proj_t.reshape((pairs, 2, width, tokens)), 0, me // 2), 1, me % 2)
        near = near.transpose(1, 0, 2, 3).reshape((2 * pairs * width, tokens))
        both = jnp.stack(products(near, act_proj_t)).reshape((2, 2, pairs, width, rows))
        total = both[:, 0] + flip(both[:, 1].astype(BF16), "dp", 1).astype(F32)
        ours = [total[:, r].astype(BF16) for r in range(pairs)]
    total = ours[0].astype(F32)
    for r in range(1, pairs):
        total += flip(ours[r], "dp", 2 * r).astype(F32)
    total += flip(total.astype(BF16), "dp", blocks).astype(F32)
    return total[0], total[1]


def gather_scaled(scaled, diag):
    pairs = lax.axis_size("dp") // 4
    x = gather_near_first(scaled, "mp")
    x = jnp.stack([x] + [flip(x, "dp", 2 * r) for r in range(1, pairs)])
    x, diag = lax.optimization_barrier((x, diag))
    return x, flip(x, "dp", 1), diag


def place_diag(diag_t):
    n_dp, n_mp = lax.axis_size("dp"), lax.axis_size("mp")
    width, rows = diag_t.shape[0], diag_t.shape[1] // n_mp
    share, blocks = n_mp // 2, n_dp // 2
    here, me = lax.axis_index("mp"), lax.axis_index("dp")
    block = here * blocks + me % blocks
    out = jnp.zeros((share, width, rows), diag_t.dtype)
    for k in range(share):
        hops = []
        for m in range(n_mp):
            for i in range(n_dp):
                b = m * blocks + i % blocks
                hops.append((i * n_mp + m, (b // share) * n_mp + 2 * ((b + k) % share) + i // blocks))
        target = 2 * ((block + k) % share) + me // blocks
        sent = lax.dynamic_slice(diag_t, (0, target * rows), (width, rows))
        got = lax.ppermute(sent, ("dp", "mp"), hops)
        out = lax.dynamic_update_slice(out, got[None], ((here // 2 - k) % share, 0, 0))
    return out.reshape((share * width, rows))


def on_device(acts, grads, basis_in, basis_out, damping):
    tok_rows = acts.shape[0]
    n_dp, n_mp = lax.axis_size("dp"), lax.axis_size("mp")
    me = lax.axis_index("dp")
    tokens_all = tok_rows * n_dp
    out_units, directions = basis_out.shape
    width = directions // n_dp

    core, half = me % 2, n_dp // 2
    units = acts.shape[1]
    chunks = units // 2 // out_units
    own_rows = basis_in.shape[1]
    mine = basis_in.T

    def side_of(side):
        part = lax.dynamic_slice(mine, (0, side * (units // 2)), (own_rows, units // 2))
        return jnp.stack([part[:, c * out_units : (c + 1) * out_units] for c in range(chunks)])

    kept = side_of(core)
    got = flip(side_of(1 - core), "dp", 1)
    both = jnp.stack([jnp.where(core == 0, kept, got), jnp.where(core == 0, got, kept)], axis=1)
    rows = 2 * own_rows
    in_rows = chunks * rows
    basis_out_t = basis_out.T
    own_piece = jnp.concatenate([both.reshape((in_rows, out_units)), basis_out_t])

    wide_grads = gather_doubling(grads, "mp")

    ahead, back_hops = ring_hops(n_dp)
    everyone = (ahead[0] + back_hops[1], back_hops[0] + ahead[1])
    began = ring_place("dp")
    grad_proj_t = jnp.zeros((directions, tok_rows), F32)
    owns, others, pairs, sums, gots = [], [], [], [], []
    rows_near = basis_out_t

    def take_grads(pieces, where_from):
        nonlocal grad_proj_t
        origins = [2 * p + core for p in where_from] + [2 * p + 1 - core for p in where_from]
        grad_proj_t = add_grads(pieces, origins, wide_grads, grad_proj_t, n_dp)

    def use(pieces, where_from, grads_too=True, costed=False, known=()):
        fresh = [flip(piece, "dp", 1) for piece in pieces[len(known) :]]
        swapped = list(known) + fresh[::-1]
        sums.append(project(pieces, swapped, rows, core, acts, costed))
        gots.append([flip(sums[-1].astype(BF16), "mp", 1)] if n_mp == 2 else [])
        owns.extend(pieces)
        others.extend(swapped)
        pairs.extend(where_from)
        if grads_too:
            take_grads(pieces + swapped, where_from)

    moving = [own_piece, own_piece]
    waiting = [own_piece], [me // 2]
    for step in range(1, half // 2):
        moving = [lax.ppermute(x, "dp", everyone[k]) for k, x in enumerate(moving)]
        if step == 1:
            swapped = flip(own_piece, "dp", 1)
            moving, own_piece, swapped = lax.optimization_barrier((moving, own_piece, swapped))
            waiting = [own_piece], [me // 2]
        else:
            use(*waiting, known=[swapped] if step == 2 else [])
            moving, sums[-1], gots[:-1], grad_proj_t, rows_near = lax.optimization_barrier(
                (moving, sums[-1], gots[:-1], grad_proj_t, rows_near)
            )
            waiting = [], []
        if step == min(2, half // 2 - 1):
            rows_near = gather_near_first(rows_near, "mp")
        way = (1 - 2 * core) * step
        waiting = waiting[0] + moving, waiting[1] + [began(way), began(-way)]

    last = lax.ppermute(moving[0][:in_rows], "dp", everyone[0])
    held = moving[0][in_rows:]
    use(*waiting)
    held, last, sums[-1], gots[:-1], grad_proj_t = lax.optimization_barrier(
        (held, last, sums[-1], gots[:-1], grad_proj_t)
    )
    last_out = lax.ppermute(held, "dp", everyone[0])
    last_pair = began(half // 2)
    use([last], [last_pair], False, True)
    last_out, sums[-1], gots[:-1] = lax.optimization_barrier((last_out, sums[-1], gots[:-1]))
    grad_proj_t = add_grads(
        [last_out, flip(last_out, "dp", 1)],
        [2 * last_pair + core, 2 * last_pair + 1 - core],
        wide_grads,
        grad_proj_t,
        n_dp,
        True,
    )

    rows_near = rows_near.reshape((n_mp, half // 2, 2, 2 * width, out_units))
    rows_near = near_first(near_first(rows_near, 1, (me // 2) % (half // 2)), 2, core)
    rows_near = rows_near.transpose(2, 1, 0, 3, 4).reshape((n_mp * directions, out_units))

    rotated, squares = token_sums(
        grad_proj_t.reshape((half, 2 * width, tok_rows)), sums, [got for part in gots for got in part], pairs, rows
    )
    diag_t = squares / tokens_all
    scaled = (rotated / (diag_t + damping[0])).astype(BF16)
    near, far, diag = gather_scaled(scaled, place_diag(diag_t))
    near, far = (x.reshape((directions * n_mp // 2, -1)) for x in (near, far))
    update, diag_t = expand(owns, others, pairs, rows, units, core, near, far, rows_near, diag)
    return (update, diag_t.T)


def solution(mesh):
    placed = (P("dp", "mp"), P("dp", "mp"), P("mp", "dp"), P("dp", "mp"), P())
    return jax.shard_map(
        on_device,
        mesh=mesh,
        in_specs=placed,
        out_specs=(P("mp", "dp"), P("mp", "dp")),
        check_vma=False,
    )
```

```python
import functools

import jax
import jax.numpy as jnp
from jax import lax
from jax.experimental import pallas as pl
from jax.experimental.pallas import tpu as pltpu
from jax.sharding import PartitionSpec as P

BF16, F32 = jnp.bfloat16, jnp.float32
VMEM_BYTES = 48 * 1024 * 1024
FIRST = 2
AHEAD = 3
PROJECT_UNITS = 8192


def flip(x, axis_name, bit):
    size = lax.axis_size(axis_name)
    return lax.ppermute(x, axis_name, [(i, i ^ bit) for i in range(size)])


def bits(axis_name):
    size = lax.axis_size(axis_name)
    assert size & (size - 1) == 0
    return [1 << k for k in range(size.bit_length() - 1)]


def gather_doubling(x, axis_name):
    me = lax.axis_index(axis_name)
    x = x[None]
    for bit in reversed(bits(axis_name)):
        other = flip(x, axis_name, bit)
        side = (me // bit) % 2
        low = jnp.where(side == 0, x, other)
        high = jnp.where(side == 0, other, x)
        x = jnp.stack([low, high], axis=1).reshape((2 * x.shape[0],) + x.shape[1:])
    return x


def ring_hops(size):
    half = size // 2
    order = list(range(0, half, 2)) + list(range(half - 1, 0, -2))
    hops = [(order[k], order[(k + 1) % half]) for k in range(half)]
    ahead = [[(2 * s + c, 2 * d + c) for s, d in hops] for c in (0, 1)]
    return ahead, [[(d, s) for s, d in part] for part in ahead]


def ring_place(axis_name):
    half = lax.axis_size(axis_name) // 2
    pair = lax.axis_index(axis_name) // 2
    place = jnp.where(pair % 2 == 0, pair // 2, half - (pair + 1) // 2)

    def began(step):
        p = (place - step) % half
        return jnp.where(p < half // 2, 2 * p, 2 * (half - p) - 1)

    return began


def tile_of(extent, most):
    return max(t for t in range(128, most + 1, 128) if extent % t == 0)


def whole_block(shape):
    return pl.BlockSpec(shape, lambda *_: (0,) * len(shape))


def halves_spec(shape, tiles, second):
    if second:
        return pl.BlockSpec(shape, lambda i, *_: (jnp.maximum(i - tiles, 0), 0))
    return pl.BlockSpec(shape, lambda i, *_: (jnp.minimum(i, tiles - 1), 0))


def tile_index(i, tiles, at_ref):
    return jnp.where(i < tiles, at_ref[0], 1 - at_ref[0]) * tiles + i % tiles


def project_kernel(tiles, rows, at_ref, acts_ref, *refs):
    sums_ref, held = refs[-2:]
    count = len(refs) // 2 - 1
    step = pl.program_id(0)
    lanes = refs[0].shape[1]

    @pl.when(step == 0)
    def _():
        held[...] = jnp.zeros_like(held)

    def add(pieces):
        total = held[...]
        for c in range(pieces[0].shape[0] // rows):
            part = jnp.concatenate([piece[c * rows : (c + 1) * rows] for piece in pieces], axis=0)
            total += lax.dot_general(
                acts_ref[:, c * lanes : (c + 1) * lanes],
                part,
                (((1,), (1,)), ((), ())),
                preferred_element_type=F32,
            )
        held[...] = total

    pl.when(step < tiles)(lambda: add(refs[:count]))
    pl.when(step >= tiles)(lambda: add(refs[count:-2]))

    @pl.when(step == 2 * tiles - 1)
    def _():
        sums_ref[...] = held[...].T


def project(owns, others, rows, core, acts, costed=False):
    tokens, units = acts.shape
    lanes = owns[0].shape[1]
    chunks = units // 2 // lanes
    if rows % 16:
        total = 0
        for pieces, side in ((owns, core), (others, 1 - core)):
            half = lax.dynamic_slice(acts, (0, side * (units // 2)), (tokens, units // 2))
            plain = [unchunk(piece, rows, chunks) for piece in pieces]
            total += jnp.concatenate(
                [lax.dot_general(p, half, (((1,), (1,)), ((), ())), preferred_element_type=F32) for p in plain]
            )
        return total
    group = max(g for g in range(1, chunks + 1) if chunks % g == 0 and g * lanes <= PROJECT_UNITS)
    tiles = chunks // group
    return pl.pallas_call(
        functools.partial(project_kernel, tiles, rows),
        grid_spec=pltpu.PrefetchScalarGridSpec(
            num_scalar_prefetch=1,
            grid=(2 * tiles,),
            in_specs=[pl.BlockSpec((tokens, group * lanes), lambda i, at_ref: (0, tile_index(i, tiles, at_ref)))]
            + [halves_spec((group * rows, lanes), tiles, False)] * len(owns)
            + [halves_spec((group * rows, lanes), tiles, True)] * len(owns),
            out_specs=whole_block((len(owns) * rows, tokens)),
            scratch_shapes=[pltpu.VMEM((tokens, len(owns) * rows), F32)],
        ),
        out_shape=jax.ShapeDtypeStruct((len(owns) * rows, tokens), F32),
        compiler_params=pltpu.CompilerParams(vmem_limit_bytes=VMEM_BYTES),
        cost_estimate=pl.CostEstimate(
            flops=2 * len(owns) * rows * units * tokens if costed else 1,
            bytes_accessed=2 * units * (len(owns) * rows + tokens) if costed else 1,
            transcendentals=0,
        ),
        name="project_acts",
    )(core.astype(jnp.int32).reshape((1,)), acts, *owns, *others)


def unchunk(piece, rows, chunks):
    lanes = piece.shape[1]
    return piece[: chunks * rows].reshape((chunks, rows, lanes)).transpose(1, 0, 2).reshape((rows, -1))


def add_grads_kernel(apart, at_ref, *refs):
    total_ref, out_ref, held, arrived = refs[-4:]
    count = (len(refs) - 4) // 2
    copies = []
    if apart:
        early = pltpu.make_async_copy(total_ref, out_ref, arrived.at[count])
        early.start()
    for k in range(count):
        start = refs[k].shape[0] - held.shape[1]
        copies.append(
            pltpu.make_async_copy(refs[k].at[pl.ds(start, held.shape[1])], held.at[k], arrived.at[k])
        )
        copies[-1].start()
    total = jnp.zeros(out_ref.shape, F32) if apart else total_ref[...]
    for k in range(count):
        copies[k].wait()
        total += lax.dot_general(
            held[k], refs[count + k][0], (((1,), (1,)), ((), ())), preferred_element_type=F32
        )
    if apart:
        early.wait()
        total += out_ref[...]
    out_ref[...] = total


def add_grads(pieces, origins, wide_grads, total, n_dp, apart=False):
    directions, units = total.shape[0], pieces[0].shape[1]
    n_mp, tokens, _ = wide_grads.shape
    share = n_dp // n_mp
    count = len(pieces)
    at = jnp.stack([f(origin, share) for origin in origins for f in (jnp.floor_divide, jnp.remainder)])

    def columns(k):
        return pl.BlockSpec((1, tokens, units), lambda i, at_ref: (at_ref[2 * k], 0, at_ref[2 * k + 1]))

    return pl.pallas_call(
        functools.partial(add_grads_kernel, apart),
        grid_spec=pltpu.PrefetchScalarGridSpec(
            num_scalar_prefetch=1,
            grid=(1,),
            in_specs=[pl.BlockSpec(memory_space=pl.ANY)] * count
            + [columns(k) for k in range(count)]
            + [pl.BlockSpec(memory_space=pltpu.HBM) if apart else whole_block(total.shape)],
            out_specs=whole_block(total.shape),
            scratch_shapes=[
                pltpu.VMEM((count, directions, units), BF16),
                pltpu.SemaphoreType.DMA((count + 1,)),
            ],
        ),
        out_shape=jax.ShapeDtypeStruct(total.shape, F32),
        compiler_params=pltpu.CompilerParams(vmem_limit_bytes=VMEM_BYTES),
        cost_estimate=pl.CostEstimate(flops=1, bytes_accessed=1, transcendentals=0),
        name="add_grads",
    )(at.astype(jnp.int32), *pieces, *[wide_grads] * count, total)


def join_kernel(at_ref, early_ref, late_ref, out_ref):
    count = early_ref.shape[0]
    for k in range(count):
        out_ref[at_ref[k]] = early_ref[k]
    out_ref[at_ref[count]] = late_ref[0]


def join(early, late, at):
    whole = pl.BlockSpec(memory_space=pltpu.VMEM)
    return pl.pallas_call(
        join_kernel,
        in_specs=[pl.BlockSpec(memory_space=pltpu.SMEM), whole, whole],
        out_specs=whole,
        out_shape=jax.ShapeDtypeStruct((early.shape[0] + 1,) + early.shape[1:], early.dtype),
        name="join_pairs",
    )(at, early, late)


def expand_kernel(tiles, rows, at_ref, near_ref, far_ref, turn_ref, _, *refs):
    count = (len(refs) - 11) // 2
    groups, out_ref = (refs[:count], refs[count : 2 * count]), refs[2 * count]
    scaled, turned, back, held, pieces, sent, first_sem, piece_sem, out_sem = refs[-9:]
    depth, lanes = near_ref.shape[0], pieces.shape[3]
    half_units = out_ref.shape[0] // 2

    def fetch(n):
        half, first, chunks = tiles[n]
        part = pl.ds(first * rows, chunks * rows)
        return [
            pltpu.make_async_copy(ref.at[part], pieces.at[half, k, part], piece_sem.at[n, k])
            for k, ref in enumerate(groups[half])
        ]

    def store(n):
        half, first, chunks = tiles[n]
        side = at_ref[0] if half == 0 else 1 - at_ref[0]
        return pltpu.make_async_copy(
            sent.at[n % 2, pl.ds(0, chunks * lanes)],
            out_ref.at[pl.ds(side * half_units + first * lanes, chunks * lanes)],
            out_sem.at[n % 2],
        )

    opening = [
        pltpu.make_async_copy(near_ref, scaled.at[0], first_sem.at[0]),
        pltpu.make_async_copy(far_ref, scaled.at[1], first_sem.at[1]),
        pltpu.make_async_copy(turn_ref, turned, first_sem.at[2]),
    ]
    for copy in opening + fetch(0):
        copy.start()
    for copy in opening:
        copy.wait()
    for n in range(1, AHEAD):
        for copy in fetch(n):
            copy.start()
    dims = (((0,), (0,)), ((), ()))
    total = lax.dot_general(scaled[0], turned[:depth], dims, preferred_element_type=F32)
    total += lax.dot_general(scaled[1], turned[depth:], dims, preferred_element_type=F32)
    back[...] = total.astype(BF16)
    for k in range(count):
        start = pl.multiple_of(at_ref[1 + k] * rows, 16)
        held[k * rows : (k + 1) * rows] = back[pl.ds(start, rows)]

    for n, (half, first, chunks) in enumerate(tiles):
        if n + AHEAD < len(tiles):
            for copy in fetch(n + AHEAD):
                copy.start()
        for copy in fetch(n):
            copy.wait()
        if n >= 2:
            store(n - 2).wait()
        for c in range(chunks):
            at = (first + c) * rows
            part = jnp.concatenate([pieces[half, k, at : at + rows] for k in range(count)], axis=0)
            sent[n % 2, c * lanes : (c + 1) * lanes] = lax.dot_general(
                part, held[...], dims, preferred_element_type=F32
            ).astype(BF16)
        store(n).start()
    store(len(tiles) - 2).wait()
    store(len(tiles) - 1).wait()


def expand(owns, others, pairs, rows, units, core, near, far, turn, diag_t):
    lanes = owns[0].shape[1]
    chunks = units // 2 // lanes
    columns = turn.shape[1]
    at = jnp.stack([core] + list(pairs)).astype(jnp.int32)
    if rows % 16:
        wide = jnp.concatenate([near, far])
        back = lax.dot_general(wide, turn, (((0,), (0,)), ((), ())), preferred_element_type=F32).astype(BF16)
        held = jnp.take(back.reshape((-1, rows, columns)), at[1:], axis=0).reshape((-1, columns))
        sides = []
        for pieces in (owns, others):
            plain = jnp.concatenate([unchunk(piece, rows, chunks) for piece in pieces])
            sides.append(lax.dot_general(plain, held, (((0,), (0,)), ((), ())), preferred_element_type=F32).astype(BF16))
        return jnp.where(core == 0, jnp.concatenate(sides), jnp.concatenate(sides[::-1])), diag_t
    size = max(1, (chunks - FIRST) // 2)
    cuts = sorted({0, min(FIRST, chunks)} | set(range(FIRST, chunks, size)) | {chunks})
    spans = [(low, high - low) for low, high in zip(cuts, cuts[1:])]
    tiles = [(0, low, n) for low, n in spans] + [(1, chunks - low - n, n) for low, n in spans[::-1]]
    count = len(owns)
    anywhere = pl.BlockSpec(memory_space=pl.ANY)
    return pl.pallas_call(
        functools.partial(expand_kernel, tiles, rows),
        grid_spec=pltpu.PrefetchScalarGridSpec(
            num_scalar_prefetch=1,
            grid=(1,),
            in_specs=[anywhere] * 3 + [pl.BlockSpec(memory_space=pltpu.HBM)] + [anywhere] * (2 * count),
            out_specs=[anywhere, pl.BlockSpec(memory_space=pltpu.HBM)],
            scratch_shapes=[
                pltpu.VMEM((2,) + near.shape, BF16),
                pltpu.VMEM(turn.shape, BF16),
                pltpu.VMEM((count * rows, columns), BF16),
                pltpu.VMEM((count * rows, columns), BF16),
                pltpu.VMEM((2, count, chunks * rows, lanes), BF16),
                pltpu.VMEM((2, max(n for _, _, n in tiles) * lanes, columns), BF16),
                pltpu.SemaphoreType.DMA((3,)),
                pltpu.SemaphoreType.DMA((len(tiles), count)),
                pltpu.SemaphoreType.DMA((2,)),
            ],
        ),
        out_shape=[jax.ShapeDtypeStruct((units, columns), BF16), jax.ShapeDtypeStruct(diag_t.shape, F32)],
        input_output_aliases={4: 1},
        compiler_params=pltpu.CompilerParams(vmem_limit_bytes=VMEM_BYTES),
        cost_estimate=pl.CostEstimate(
            flops=2 * rows * count * units * columns, bytes_accessed=2 * units * columns, transcendentals=0
        ),
        name="expand_update",
    )(at, near, far, turn, diag_t, *owns, *others)


def gather_near_first(x, axis_name):
    x = x[None]
    for bit in bits(axis_name):
        x = jnp.concatenate([x, flip(x, axis_name, bit)], axis=0)
    return x


def near_first(x, axis, me):
    size = x.shape[axis]
    for k in range(size.bit_length() - 1):
        shape = x.shape[:axis] + (size >> (k + 1), 2, 1 << k) + x.shape[axis + 1 :]
        parts = x.reshape(shape)
        swapped = jnp.flip(parts, axis + 1)
        x = jnp.where((me >> k) % 2 == 1, swapped, parts).reshape(x.shape)
    return x


def products(g, a):
    dims = (((1,), (1,)), ((), ()))
    g = g.astype(BF16)
    g_sq = (g.astype(F32) ** 2).astype(BF16)
    a_sq = (a.astype(F32) ** 2).astype(BF16)
    return (
        lax.dot_general(g, a, dims, preferred_element_type=F32),
        lax.dot_general(g_sq, a_sq, dims, preferred_element_type=F32),
    )


def picked(me_ref, g_ref, flipped):
    pairs = g_ref.shape[0] // 2
    core, pair = me_ref[0] % 2, me_ref[0] // 2
    return jnp.concatenate(
        [g_ref[(pair ^ r) * 2 + (core ^ flipped)] for r in range(pairs)], axis=0
    )


def theirs_kernel(rows, me_ref, at_ref, g_ref, *refs):
    out_ref, a_ref = refs[-2:]
    count = len(refs) // 2 - 1
    k = 0
    for own_ref, got_ref in zip(refs[:count], refs[count:-2]):
        total = (own_ref[...] + got_ref[...].astype(F32)).astype(BF16)
        for i in range(total.shape[0] // rows):
            start = pl.multiple_of(at_ref[k] * rows, 16)
            a_ref[pl.ds(start, rows)] = total[i * rows : (i + 1) * rows]
            k += 1
    rotated, squares = products(picked(me_ref, g_ref, 1), a_ref[...])
    out_ref[0] = rotated.astype(BF16)
    out_ref[1] = squares.astype(BF16)


def ours_kernel(me_ref, g_ref, a_ref, got_ref, *out_refs):
    width = g_ref.shape[1]
    rotated, squares = products(picked(me_ref, g_ref, 0), a_ref[...])
    rotated += got_ref[0].astype(F32)
    squares += got_ref[1].astype(F32)
    pairs = len(out_refs) // 2
    for r in range(pairs):
        out_refs[r][...] = rotated[r * width : (r + 1) * width].astype(BF16)
        out_refs[pairs + r][...] = squares[r * width : (r + 1) * width].astype(BF16)


def token_sums(grad_proj_t, sums, gots, order, pair_rows):
    blocks, width, tokens = grad_proj_t.shape
    pairs = blocks // 2
    top = lax.axis_size("dp") // blocks
    assert top == 2
    rows = len(order) * pair_rows
    order = jnp.stack(order).astype(jnp.int32)
    me = lax.axis_index("dp") % blocks
    whole = pl.BlockSpec(memory_space=pltpu.VMEM)
    if width % 16 == 0 and pair_rows % 16 == 0 and gots:
        params = pltpu.CompilerParams(vmem_limit_bytes=VMEM_BYTES)
        cost = pl.CostEstimate(
            flops=2 * blocks * width * rows * tokens,
            bytes_accessed=4 * blocks * width * tokens + 2 * rows * tokens + 2 * blocks * width * rows,
            transcendentals=0,
        )
        index = me.astype(jnp.int32).reshape((1,))
        index_spec = pl.BlockSpec(memory_space=pltpu.SMEM)
        sent, act_proj_t = pl.pallas_call(
            functools.partial(theirs_kernel, pair_rows),
            in_specs=[index_spec, index_spec, whole] + [whole] * (len(sums) + len(gots)),
            out_specs=[whole, whole],
            out_shape=[
                jax.ShapeDtypeStruct((2, pairs * width, rows), BF16),
                jax.ShapeDtypeStruct((rows, tokens), BF16),
            ],
            compiler_params=params,
            cost_estimate=cost,
            name="sums_for_other_core",
        )(index, order, grad_proj_t, *sums, *gots)
        got = flip(sent, "dp", 1)
        ours = pl.pallas_call(
            ours_kernel,
            in_specs=[index_spec, whole, whole, whole],
            out_specs=[whole] * (2 * pairs),
            out_shape=[jax.ShapeDtypeStruct((width, rows), BF16)] * (2 * pairs),
            compiler_params=params,
            cost_estimate=cost,
            name="sums_for_own_core",
        )(index, grad_proj_t, act_proj_t, got)
    else:
        act_proj_t = jnp.concatenate(sums)
        for bit in bits("mp"):
            act_proj_t = act_proj_t + flip(act_proj_t.astype(BF16), "mp", bit).astype(F32)
        act_proj_t = act_proj_t.astype(BF16).reshape((-1, pair_rows, tokens))
        act_proj_t = join(act_proj_t[:-1], act_proj_t[-1:], order).reshape((-1, tokens))
        near = near_first(near_first(grad_proj_t.reshape((pairs, 2, width, tokens)), 0, me // 2), 1, me % 2)
        near = near.transpose(1, 0, 2, 3).reshape((2 * pairs * width, tokens))
        both = jnp.stack(products(near, act_proj_t)).reshape((2, 2, pairs, width, rows))
        total = both[:, 0] + flip(both[:, 1].astype(BF16), "dp", 1).astype(F32)
        ours = [total[part, r].astype(BF16) for part in range(2) for r in range(pairs)]
    totals = []
    for part in (ours[:pairs], ours[pairs:]):
        total = part[0].astype(F32)
        for r in range(1, pairs):
            total += flip(part[r], "dp", 2 * r).astype(F32)
        totals.append(total + flip(total.astype(BF16), "dp", blocks).astype(F32))
    return totals[0], totals[1]


def gather_scaled(scaled, diag):
    pairs = lax.axis_size("dp") // 4
    x = gather_near_first(scaled, "mp")
    x = jnp.stack([x] + [flip(x, "dp", 2 * r) for r in range(1, pairs)])
    x, diag = lax.optimization_barrier((x, diag))
    return x, flip(x, "dp", 1), diag


def place_diag(diag_t):
    n_dp, n_mp = lax.axis_size("dp"), lax.axis_size("mp")
    width, rows = diag_t.shape[0], diag_t.shape[1] // n_mp
    share, blocks = n_mp // 2, n_dp // 2
    here, me = lax.axis_index("mp"), lax.axis_index("dp")
    block = here * blocks + me % blocks
    out = jnp.zeros((share, width, rows), diag_t.dtype)
    for k in range(share):
        hops = []
        for m in range(n_mp):
            for i in range(n_dp):
                b = m * blocks + i % blocks
                hops.append((i * n_mp + m, (b // share) * n_mp + 2 * ((b + k) % share) + i // blocks))
        target = 2 * ((block + k) % share) + me // blocks
        sent = lax.dynamic_slice(diag_t, (0, target * rows), (width, rows))
        got = lax.ppermute(sent, ("dp", "mp"), hops)
        out = lax.dynamic_update_slice(out, got[None], ((here // 2 - k) % share, 0, 0))
    return out.reshape((share * width, rows))


def on_device(acts, grads, basis_in, basis_out, damping):
    tok_rows = acts.shape[0]
    n_dp, n_mp = lax.axis_size("dp"), lax.axis_size("mp")
    me = lax.axis_index("dp")
    tokens_all = tok_rows * n_dp
    out_units, directions = basis_out.shape
    width = directions // n_dp

    core, half = me % 2, n_dp // 2
    units = acts.shape[1]
    chunks = units // 2 // out_units
    own_rows = basis_in.shape[1]
    mine = basis_in.T

    def side_of(side):
        part = lax.dynamic_slice(mine, (0, side * (units // 2)), (own_rows, units // 2))
        return jnp.stack([part[:, c * out_units : (c + 1) * out_units] for c in range(chunks)])

    kept = side_of(core)
    got = flip(side_of(1 - core), "dp", 1)
    both = jnp.stack([jnp.where(core == 0, kept, got), jnp.where(core == 0, got, kept)], axis=1)
    rows = 2 * own_rows
    in_rows = chunks * rows
    basis_out_t = basis_out.T
    own_piece = jnp.concatenate([both.reshape((in_rows, out_units)), basis_out_t])

    wide_grads = gather_doubling(grads, "mp")

    ahead, back_hops = ring_hops(n_dp)
    everyone = (ahead[0] + back_hops[1], back_hops[0] + ahead[1])
    began = ring_place("dp")
    grad_proj_t = jnp.zeros((directions, tok_rows), F32)
    owns, others, pairs, sums, gots = [], [], [], [], []
    rows_near = basis_out_t

    def take_grads(pieces, where_from):
        nonlocal grad_proj_t
        origins = [2 * p + core for p in where_from] + [2 * p + 1 - core for p in where_from]
        grad_proj_t = add_grads(pieces, origins, wide_grads, grad_proj_t, n_dp)

    def use(pieces, where_from, grads_too=True, costed=False, known=()):
        fresh = [flip(piece, "dp", 1) for piece in pieces[len(known) :]]
        swapped = list(known) + fresh[::-1]
        sums.append(project(pieces, swapped, rows, core, acts, costed))
        gots.append([flip(sums[-1].astype(BF16), "mp", 1)] if n_mp == 2 else [])
        owns.extend(pieces)
        others.extend(swapped)
        pairs.extend(where_from)
        if grads_too:
            take_grads(pieces + swapped, where_from)

    moving = [own_piece, own_piece]
    waiting = [own_piece], [me // 2]
    for step in range(1, half // 2):
        moving = [lax.ppermute(x, "dp", everyone[k]) for k, x in enumerate(moving)]
        if step == 1:
            swapped = flip(own_piece, "dp", 1)
            moving, own_piece, swapped = lax.optimization_barrier((moving, own_piece, swapped))
            waiting = [own_piece], [me // 2]
        else:
            use(*waiting, known=[swapped] if step == 2 else [])
            moving, sums[-1], gots[:-1], grad_proj_t, rows_near = lax.optimization_barrier(
                (moving, sums[-1], gots[:-1], grad_proj_t, rows_near)
            )
            waiting = [], []
        if step == min(2, half // 2 - 1):
            rows_near = gather_near_first(rows_near, "mp")
        way = (1 - 2 * core) * step
        waiting = waiting[0] + moving, waiting[1] + [began(way), began(-way)]

    last = lax.ppermute(moving[0][:in_rows], "dp", everyone[0])
    held = moving[0][in_rows:]
    use(*waiting)
    held, last, sums[-1], gots[:-1], grad_proj_t = lax.optimization_barrier(
        (held, last, sums[-1], gots[:-1], grad_proj_t)
    )
    last_out = lax.ppermute(held, "dp", everyone[0])
    last_pair = began(half // 2)
    use([last], [last_pair], False, True)
    last_out, sums[-1], gots[:-1] = lax.optimization_barrier((last_out, sums[-1], gots[:-1]))
    grad_proj_t = add_grads(
        [last_out, flip(last_out, "dp", 1)],
        [2 * last_pair + core, 2 * last_pair + 1 - core],
        wide_grads,
        grad_proj_t,
        n_dp,
        True,
    )

    rows_near = rows_near.reshape((n_mp, half // 2, 2, 2 * width, out_units))
    rows_near = near_first(near_first(rows_near, 1, (me // 2) % (half // 2)), 2, core)
    rows_near = rows_near.transpose(2, 1, 0, 3, 4).reshape((n_mp * directions, out_units))

    rotated, squares = token_sums(
        grad_proj_t.reshape((half, 2 * width, tok_rows)), sums, [got for part in gots for got in part], pairs, rows
    )
    diag_t = squares / tokens_all
    scaled = (rotated / (diag_t + damping[0])).astype(BF16)
    near, far, diag = gather_scaled(scaled, place_diag(diag_t))
    near, far = (x.reshape((directions * n_mp // 2, -1)) for x in (near, far))
    update, diag_t = expand(owns, others, pairs, rows, units, core, near, far, rows_near, diag)
    return (update, diag_t.T)


def solution(mesh):
    placed = (P("dp", "mp"), P("dp", "mp"), P("mp", "dp"), P("dp", "mp"), P())
    return jax.shard_map(
        on_device,
        mesh=mesh,
        in_specs=placed,
        out_specs=(P("mp", "dp"), P("mp", "dp")),
        check_vma=False,
    )
```
